256 devices in a mesh: dp: 8 (over y, core), cent: 32 (over x, z).
Axes of the slice: x: 4, y: 4, z: 8, core: 2. Of those that a mesh axis runs over, the one named last changes fastest.
Arguments:
- batch: bfloat16 [2, 32768, 768], P(None, ('dp', 'cent')), may hold values from -16 to 16
- centroids: float32 [16384, 768], P('cent'), may hold values from -0.25 to 0.25
- counts: float32 [16384], P('cent'), may hold values from 4 to 32
Outputs:
- refined_centroids: float32 [16384, 768], P('cent')
- new_counts: float32 [16384], P('cent')
The draws below stay inside these ranges and needn't reach their ends.
All inputs are finite; a program needn't handle non-finite values.
Results may differ from the reference program's by a relative error of at most 0.011.
Values may be sent and summed in bfloat16 or wider, within the bound.
A program may use at most 128 MiB of HBM per device.

```python
import math
import jax
import jax.numpy as jnp
from jax import lax

D = 768
STEPS = 2
CENTROIDS = 16384
BATCH = 32768


def shared_centroids(key):
    value_entries = jax.random.normal(jax.random.fold_in(key, 11), (CENTROIDS, D), jnp.float32)
    scaled = jnp.clip(value_entries, -6.0, 6.0) / jnp.sqrt(jnp.float32(D))
    return jnp.clip(scaled, -0.25, 0.25)


def draw_centroids(key, part):
    base = shared_centroids(key)
    return base


def draw_batch(key, part):
    key = jax.random.fold_in(key, 3)
    value_entries = jnp.clip(jax.random.normal(key, (STEPS, BATCH, D), jnp.float32), -6.0, 6.0)
    return value_entries.astype(jnp.bfloat16)


def steps_of(own_key, extent, shards, least, high):
    loudness, own = 1.0, jax.random.fold_in(own_key, 6)
    for dim, blocks in shards:
        draws = jnp.exp(jax.random.uniform(jax.random.fold_in(own, dim), (blocks,), jnp.float32, least / len(shards), high / len(shards)))
        loudness = loudness * jnp.repeat(draws, extent[dim] // blocks).reshape([-1 if axis == dim else 1 for axis in range(len(extent))])
    return loudness


def setup_inputs(seed: int = 0) -> dict:
    streams_of = jax.random.split(jax.random.key(seed), 4)
    batch = draw_batch(jax.random.fold_in(streams_of[3], 71), 0)
    centroids = draw_centroids(jax.random.fold_in(streams_of[3], 71), 0)
    counts = jnp.clip(jnp.exp(math.log(32.0) - 2.0794415 * jax.random.uniform(streams_of[2], (CENTROIDS,), jnp.float32) ** steps_of(streams_of[2], (CENTROIDS,), ((0, 32),), -0.2, 0.2)), 4.0, 32.0)
    return {"batch": batch, "centroids": centroids, "counts": counts}


sharpness_factor = 4.0


def reference(batch, centroids, counts):
    current = centroids
    mass = counts
    block = math.gcd(BATCH, 2048)
    for step in range(STEPS):
        quantized_values = current.astype(jnp.bfloat16)
        blocks = batch[step].reshape(BATCH // block, block, D)

        def accumulate(carry, input_rows):
            affinity_scores = jnp.dot(input_rows, quantized_values.T, preferred_element_type=jnp.float32) * sharpness_factor
            peak = jnp.max(affinity_scores, axis=1, keepdims=True)
            powers = jnp.exp(affinity_scores - peak)
            total = jnp.sum(powers, axis=1, keepdims=True)
            resp = (powers / total).astype(jnp.bfloat16)
            sums = carry[0] + jnp.dot(resp.T, input_rows, preferred_element_type=jnp.float32)
            gained = carry[1] + jnp.sum(resp.astype(jnp.float32), axis=0)
            return (sums, gained), None

        start = (jnp.zeros((CENTROIDS, D), jnp.float32), jnp.zeros((CENTROIDS,), jnp.float32))
        (sums, gained), unused = lax.scan(accumulate, start, blocks)
        current = (mass[:, None] * current + sums) / (mass + gained)[:, None]
        mass = mass + gained
    return current, mass
```

```python
import jax
import jax.numpy as jnp
from jax import lax
from jax.experimental import pallas as pl
from jax.experimental.pallas import tpu as pltpu
from jax.sharding import PartitionSpec as P

MESH = pl.DeviceIdType.MESH
F32 = jnp.float32
BF16 = jnp.bfloat16
SHARP = 4.0

NX, NY, NZ = 4, 4, 8
OWN = 128
ROWS = NZ * OWN
D = 768
HALF = D // 2
BLOCK = 512
PART = BLOCK // 2
QUART = PART // NY
SEMS = 176


def kernel(batch, cents, counts, out, new_counts, rows, cbuf, pbuf, mst, lst, stats, own_sums, csend, crecv, abuf, arecv,
           bbuf, brecv, a2, a2recv, b2, b2recv, gbuf, grecv, gsum, g1recv, g2, g2recv, cur, massbuf, send_sem, recv_sem):
    dp = lax.axis_index("dp")
    ce = lax.axis_index("cent")
    y, k = dp // 2, dp % 2
    x, z = ce // NZ, ce % NZ

    def at(px, py, pz, pk):
        return (py * 2 + pk, px * NZ + pz)

    other = at(x, y, z, 1 - k)

    def xpeer(d):
        return at((x + d) % NX, y, z, k)

    def ypeer(d):
        return at(x, (y + d) % NY, z, k)

    def zpeer(d):
        return at(x, y, (z + d) % NZ, k)

    used = [0]
    sent = []

    def take(n=1):
        used[0] += n
        return used[0] - n

    def copy(src, dst, peer, sem):
        return pltpu.make_async_remote_copy(
            src_ref=src, dst_ref=dst, send_sem=send_sem.at[sem], recv_sem=recv_sem.at[sem],
            device_id=peer, device_id_type=MESH)

    def send(src, dst, peer):
        c = copy(src, dst, peer, take())
        c.start()
        sent.append(c)
        return c

    barrier = pltpu.get_barrier_semaphore()
    peers = [other]
    peers += [xpeer(d) for d in range(1, NX)]
    peers += [ypeer(d) for d in range(1, NY)]
    peers += [zpeer(d) for d in range(1, NZ)]
    for p in peers:
        pl.semaphore_signal(barrier, inc=1, device_id=p, device_id_type=MESH)

    mine = pl.ds(pl.multiple_of(z * OWN, OWN), OWN)
    for t in range(2):
        rows[t, mine, :] = batch[t]
    for h in range(2):
        cbuf[0, x, h] = (cents[h * PART:(h + 1) * PART, :] * SHARP).astype(BF16)

    pl.semaphore_wait(barrier, len(peers))

    def ring(t):
        arrived = {}

        def hop(h):
            for sign in (1, -1):
                for c in ((0, 1) if h < 4 else ((0,) if sign == 1 else (1,))):
                    if h > 1:
                        arrived.pop((h - 1, sign, c)).wait_recv()
                    owner = (z + NZ - sign * (h - 1)) % NZ
                    where = pl.ds(pl.multiple_of(owner * OWN + c * (OWN // 2), OWN // 2), OWN // 2)
                    arrived[(h, sign, c)] = send(rows.at[t, where], rows.at[t, where], zpeer(sign % NZ))

        def finish():
            for key in sorted(arrived):
                arrived.pop(key).wait_recv()

        return hop, finish

    hop, finish = ring(0)
    hop2, finish2 = ring(1)
    hop(1)
    first = [send(cbuf.at[0, x, k], cbuf.at[0, x, k], xpeer(d)) for d in range(1, NX)]
    hop(2)
    hop(3)
    hop(4)
    hop2(1)
    passed = []
    for i, d in enumerate(range(1, NX)):
        first[i].wait_recv()
        src = cbuf.at[0, (x + NX - d) % NX, k]
        passed.append(send(src, src, other))
    finish()
    for c in passed:
        c.wait_recv()

    def scores(t):
        def body(c, _):
            for h in range(2):
                s = lax.dot_general(cbuf[t, c, h], rows[t], (((1,), (1,)), ((), ())), preferred_element_type=F32)
                m = jnp.max(s, axis=0, keepdims=True)
                p = jnp.exp(s - m)
                mst[pl.ds(c * 2 + h, 1), :] = m
                lst[pl.ds(c * 2 + h, 1), :] = jnp.sum(p, axis=0, keepdims=True)
                pbuf[c, h] = p.astype(BF16)
            return 0

        lax.fori_loop(0, NX, body, 0)

    def normalise(t):
        m = mst[...]
        top = jnp.max(m, axis=0, keepdims=True)
        stats[t, z, 0:1, :] = top
        stats[t, z, 1:2, :] = jnp.sum(lst[...] * jnp.exp(m - top), axis=0, keepdims=True)
        around = [send(stats.at[t, z], stats.at[t, z], zpeer(d)) for d in range(1, NZ)]
        for c in around:
            c.wait_recv()
        peak = stats[t, 0, 0:1, :]
        for i in range(1, NZ):
            peak = jnp.maximum(peak, stats[t, i, 0:1, :])
        total = jnp.zeros_like(peak)
        for i in range(NZ):
            total = total + stats[t, i, 1:2, :] * jnp.exp(stats[t, i, 0:1, :] - peak)
        mst[...] = jnp.exp(m - peak) / total

    def reduce_sums(t, midway):
        to_core = take(NX)
        to_x = take(NX - 1)

        def core_copy(c, i):
            return copy(csend.at[t, c], crecv.at[t, c], other, to_core + i)

        def x_copy(c, i):
            return copy(abuf.at[t, c], arecv.at[t, i], at(c, y, z, k), to_x + i)

        def combine(i):
            c = (x + 1 + i) % NX
            core_copy(c, i).wait_recv()
            whole = own_sums[c] + crecv[t, c].astype(F32)
            abuf[t, c] = whole[:, :HALF].astype(BF16)
            bbuf[t, :, c] = whole[:, HALF:].astype(BF16).reshape(NY, QUART, HALF)

            @pl.when(i < NX - 1)
            def _():
                x_copy(c, i).start()

        def body(i, _):
            c = (x + 1 + i) % NX
            for h in range(2):
                resp = (pbuf[c, h].astype(F32) * mst[pl.ds(c * 2 + h, 1), :]).astype(BF16)
                pbuf[c, h] = resp
                wide = resp.astype(F32)
                acc = wide[:, :128]
                for j in range(1, ROWS // 128):
                    acc = acc + wide[:, j * 128:(j + 1) * 128]
                gbuf[t, c, h] = lax.dot_general(
                    jnp.ones((8, 128), F32), acc, (((1,), (1,)), ((), ())),
                    precision=lax.Precision.HIGHEST, preferred_element_type=F32)
            csend[t, c] = jnp.dot(pbuf[c, 1 - k], rows[t], preferred_element_type=F32).astype(BF16)
            core_copy(c, i).start()
            own_sums[c] = jnp.dot(pbuf[c, k], rows[t], preferred_element_type=F32)

            @pl.when(i > 0)
            def _():
                combine(i - 1)

            return 0

        lax.fori_loop(0, NX, body, 0)
        g_core = send(gbuf.at[t, :, 1 - k], grecv.at[t], other)
        combine(NX - 1)
        from_y = [
            send(bbuf.at[t, (y + d) % NY], brecv.at[t, d - 1], ypeer(d)) for d in range(1, NY)]
        g_core.wait_recv()
        for c in range(NX):
            gsum[t, c] = gbuf[t, c, k] + grecv[t, c]
        g_x = [send(gsum.at[t, (x + d) % NX], g1recv.at[t, d - 1], xpeer(d)) for d in range(1, NX)]
        midway()

        for i in range(NX - 1):
            x_copy((x + 1 + i) % NX, i).wait_recv()
        part_a = abuf[t, x].astype(F32)
        for i in range(NX - 1):
            part_a = part_a + arecv[t, i].astype(F32)
        a2[t] = part_a.reshape(NY, QUART, HALF)
        sends_a = []
        for d in range(1, NY):
            a2recv[t, 3 + d - 1] = a2[t, (y + d) % NY].astype(BF16)
            sends_a.append(send(a2recv.at[t, 3 + d - 1], a2recv.at[t, d - 1], ypeer(d)))
        for c in from_y:
            c.wait_recv()
        part_b = bbuf[t, y].astype(F32)
        for i in range(NY - 1):
            part_b = part_b + brecv[t, i].astype(F32)
        b2[t] = part_b
        sends_b = []
        for d in range(1, NX):
            b2recv[t, 3 + d - 1] = b2[t, (x + d) % NX].astype(BF16)
            sends_b.append(send(b2recv.at[t, 3 + d - 1], b2recv.at[t, d - 1], xpeer(d)))
        for c in g_x:
            c.wait_recv()
        g = gsum[t, x]
        for i in range(NX - 1):
            g = g + g1recv[t, i]
        g2[t] = g
        g_y = [send(g2.at[t], g2recv.at[t, d - 1], ypeer(d)) for d in range(1, NY)]
        for c in sends_a:
            c.wait_recv()
        sum_a = a2[t, y]
        for i in range(NY - 1):
            sum_a = sum_a + a2recv[t, i].astype(F32)
        for c in sends_b:
            c.wait_recv()
        sum_b = b2[t, x]
        for i in range(NX - 1):
            sum_b = sum_b + b2recv[t, i].astype(F32)
        for c in g_y:
            c.wait_recv()
        for i in range(NY - 1):
            g = g + g2recv[t, i]
        for i in range(NX):
            core_copy((x + 1 + i) % NX, i).wait_send()
        for i in range(NX - 1):
            x_copy((x + 1 + i) % NX, i).wait_send()
        return sum_a, sum_b, g

    quarter = pl.ds(pl.multiple_of(y * QUART, QUART), QUART)
    place = pl.ds(pl.multiple_of(k * PART + y * QUART, QUART), QUART)
    lane = lax.broadcasted_iota(jnp.int32, (QUART, PART), 1)
    line = lax.broadcasted_iota(jnp.int32, (QUART, PART), 0) + y * QUART
    hit = lane == line

    def column(v):
        return jnp.sum(jnp.where(hit, v[0:1, :], 0.0), axis=1, keepdims=True)

    def update(old, mass, sum_a, sum_b, g):
        m = column(mass)
        down = m + column(g)
        return (m * old[:, :HALF] + sum_a) / down, (m * old[:, HALF:] + sum_b) / down

    scores(0)
    hop2(2)
    normalise(0)
    sum_a, sum_b, g = reduce_sums(0, lambda: hop2(3))
    mass = jnp.broadcast_to(counts[pl.ds(k, 1), :], (8, PART))
    left, right = update(cents[place, :], mass, sum_a, sum_b, g)
    mass = mass + g
    massbuf[0, k] = mass
    cur[:, :HALF] = left
    cur[:, HALF:] = right
    cbuf[1, x, k, quarter, :HALF] = (left * SHARP).astype(BF16)
    cbuf[1, x, k, quarter, HALF:] = (right * SHARP).astype(BF16)

    lo, hi = pl.ds(0, HALF), pl.ds(HALF, HALF)
    own_left = cbuf.at[1, x, k, quarter, lo]
    own_right = cbuf.at[1, x, k, quarter, hi]
    left1 = [send(own_left, own_left, ypeer(d)) for d in range(1, NY)]
    right1 = [send(own_right, own_right, xpeer(d)) for d in range(1, NX)]
    hop2(4)
    for c in left1:
        c.wait_recv()
    all_left = cbuf.at[1, x, k, :, lo]
    left2 = [send(all_left, all_left, xpeer(d)) for d in range(1, NX)]
    for c in right1:
        c.wait_recv()
    all_right = cbuf.at[1, :, k, quarter, hi]
    right2 = [send(all_right, all_right, ypeer(d)) for d in range(1, NY)]
    passed = [send(all_left, all_left, other), send(all_right, all_right, other)]
    finish2()
    for i, d in enumerate(range(1, NX)):
        left2[i].wait_recv()
        src = cbuf.at[1, (x + NX - d) % NX, k, :, lo]
        passed.append(send(src, src, other))
        right2[i].wait_recv()
        src = cbuf.at[1, :, k, pl.ds(pl.multiple_of(((y + NY - d) % NY) * QUART, QUART), QUART), hi]
        passed.append(send(src, src, other))
    for c in passed:
        c.wait_recv()

    scores(1)
    normalise(1)
    sum_a, sum_b, g = reduce_sums(1, lambda: None)
    mass = massbuf[0, k]
    left, right = update(cur[...], mass, sum_a, sum_b, g)
    out[place, :HALF] = left
    out[place, HALF:] = right
    around = [send(out.at[place], out.at[place], ypeer(d)) for d in range(1, NY)]
    passed = [send(out.at[place], out.at[place], other)]
    massbuf[1, k] = mass + g
    passed.append(send(massbuf.at[1, k], massbuf.at[1, k], other))
    for i, d in enumerate(range(1, NY)):
        around[i].wait_recv()
        src = out.at[pl.ds(pl.multiple_of(k * PART + ((y + NY - d) % NY) * QUART, QUART), QUART)]
        passed.append(send(src, src, other))
    for c in passed:
        c.wait_recv()
    new_counts[0:1, :] = massbuf[1, 0, 0:1, :]
    new_counts[1:2, :] = massbuf[1, 1, 0:1, :]
    for c in sent:
        c.wait_send()
    assert used[0] <= SEMS, used[0]


def body(batch, centroids, counts):
    vmem = pl.BlockSpec(memory_space=pltpu.VMEM)
    refined, mass = pl.pallas_call(
        kernel,
        out_shape=(
            jax.ShapeDtypeStruct((BLOCK, D), F32),
            jax.ShapeDtypeStruct((2, PART), F32),
        ),
        in_specs=[vmem] * 3,
        out_specs=(vmem, vmem),
        scratch_shapes=[
            pltpu.VMEM((2, ROWS, D), BF16),
            pltpu.VMEM((2, NX, 2, PART, D), BF16),
            pltpu.VMEM((NX, 2, PART, ROWS), BF16),
            pltpu.VMEM((2 * NX, ROWS), F32),
            pltpu.VMEM((2 * NX, ROWS), F32),
            pltpu.VMEM((2, NZ, 2, ROWS), F32),
            pltpu.VMEM((NX, PART, D), F32),
            pltpu.VMEM((2, NX, PART, D), BF16),
            pltpu.VMEM((2, NX, PART, D), BF16),
            pltpu.VMEM((2, NX, PART, HALF), BF16),
            pltpu.VMEM((2, NX - 1, PART, HALF), BF16),
            pltpu.VMEM((2, NY, NX, QUART, HALF), BF16),
            pltpu.VMEM((2, NY - 1, NX, QUART, HALF), BF16),
            pltpu.VMEM((2, NY, QUART, HALF), F32),
            pltpu.VMEM((2, 6, QUART, HALF), BF16),
            pltpu.VMEM((2, NX, QUART, HALF), F32),
            pltpu.VMEM((2, 6, QUART, HALF), BF16),
            pltpu.VMEM((2, NX, 2, 8, PART), F32),
            pltpu.VMEM((2, NX, 8, PART), F32),
            pltpu.VMEM((2, NX, 8, PART), F32),
            pltpu.VMEM((2, NX - 1, 8, PART), F32),
            pltpu.VMEM((2, 8, PART), F32),
            pltpu.VMEM((2, NY - 1, 8, PART), F32),
            pltpu.VMEM((QUART, D), F32),
            pltpu.VMEM((2, 2, 8, PART), F32),
            pltpu.SemaphoreType.DMA((SEMS,)),
            pltpu.SemaphoreType.DMA((SEMS,)),
        ],
        compiler_params=pltpu.CompilerParams(
            collective_id=0, has_side_effects=True, vmem_limit_bytes=58 * 1024 * 1024
        ),
    )(batch, centroids, counts.reshape(2, PART))
    return refined, mass.reshape(BLOCK)


def solution(mesh):
    return jax.shard_map(
        body,
        mesh=mesh,
        in_specs=(P(None, ("dp", "cent"), None), P("cent", None), P("cent")),
        out_specs=(P("cent", None), P("cent")),
        check_vma=False,
    )
```

```python
import jax
import jax.numpy as jnp
from jax import lax
from jax.experimental import pallas as pl
from jax.experimental.pallas import tpu as pltpu
from jax.sharding import PartitionSpec as P

MESH = pl.DeviceIdType.MESH
F32 = jnp.float32
BF16 = jnp.bfloat16
SHARP = 4.0

NX, NY, NZ = 4, 4, 8
OWN = 128
ROWS = NZ * OWN
D = 768
BLOCK = 512
PART = BLOCK // 2
QUART = PART // NY
ITEM = QUART // 2
SHARE = 4 * ITEM
SEMS = 160


def kernel(batch, cents, counts, out, new_counts, rows, cbuf, pbuf, mst, lst, stats, sums, crecv, abuf, arecv,
           a2, a2f, a2recv, gbuf, glin, grecv, gsum, g1recv, g2, g2recv, cur, massbuf, send_sem, recv_sem):
    dp = lax.axis_index("dp")
    ce = lax.axis_index("cent")
    y, k = dp // 2, dp % 2
    x, z = ce // NZ, ce % NZ
    me = (x, y)

    def at(px, py, pz, pk):
        return (py * 2 + pk, px * NZ + pz)

    other = at(x, y, z, 1 - k)

    def xpeer(d):
        return at((x + d) % NX, y, z, k)

    def ypeer(d):
        return at(x, (y + d) % NY, z, k)

    def zpeer(d):
        return at(x, y, (z + d) % NZ, k)

    peer = (xpeer, ypeer)
    used = [0]
    sent = []

    def take(n=1):
        used[0] += n
        return used[0] - n

    def copy(src, dst, to, sem):
        return pltpu.make_async_remote_copy(
            src_ref=src, dst_ref=dst, send_sem=send_sem.at[sem], recv_sem=recv_sem.at[sem],
            device_id=to, device_id_type=MESH)

    def send(src, dst, to):
        c = copy(src, dst, to, take())
        c.start()
        sent.append(c)
        return c

    def items(i):
        return pl.ds(pl.multiple_of(i * ITEM, ITEM), ITEM)

    barrier = pltpu.get_barrier_semaphore()
    peers = [other]
    peers += [xpeer(d) for d in range(1, NX)]
    peers += [ypeer(d) for d in range(1, NY)]
    peers += [zpeer(d) for d in range(1, NZ)]
    for p in peers:
        pl.semaphore_signal(barrier, inc=1, device_id=p, device_id_type=MESH)

    mine = pl.ds(pl.multiple_of(z * OWN, OWN), OWN)
    for t in range(2):
        rows[t, mine, :] = batch[t]

    def from_block(first):
        return (cents[pl.ds(pl.multiple_of(k * PART + first, ITEM), ITEM), :] * SHARP).astype(BF16)

    for q in range(NY):
        cbuf[0, 0, x, k, q * ITEM:(q + 1) * ITEM, :] = from_block(q * QUART)
    cbuf[0, 1, y, k, items(x), :] = from_block(y * QUART + ITEM)

    pl.semaphore_wait(barrier, len(peers))

    def ring(t):
        arrived = {}

        def hop(h):
            for sign in (1, -1):
                for c in ((0, 1) if h < 4 else ((0,) if sign == 1 else (1,))):
                    if h > 1:
                        arrived.pop((h - 1, sign, c)).wait_recv()
                    owner = (z + NZ - sign * (h - 1)) % NZ
                    where = pl.ds(pl.multiple_of(owner * OWN + c * (OWN // 2), OWN // 2), OWN // 2)
                    arrived[(h, sign, c)] = send(rows.at[t, where], rows.at[t, where], zpeer(sign % NZ))

        def finish():
            for key in sorted(arrived):
                arrived.pop(key).wait_recv()

        return hop, finish

    def spread(t):
        near = take(6)
        far = take(6)
        over = take(8)

        def small(ty, d):
            src = cbuf.at[t, ty, me[ty], k, items(me[1 - ty])]
            return copy(src, src, peer[1 - ty](d), near + ty * 3 + d - 1)

        def large(ty, d):
            src = cbuf.at[t, ty, me[ty], k]
            return copy(src, src, peer[ty](d), far + ty * 3 + d - 1)

        def on(ty, d):
            src = cbuf.at[t, ty, (me[ty] + 4 - d) % 4, k]
            return copy(src, src, other, over + ty * 4 + d)

        def first(ty):
            for d in (2, 1, 3):
                small(ty, d).start()

        def second(ty, wait=True):
            if wait:
                for d in (1, 3, 2):
                    small(ty, d).wait()
            for d in (2, 1, 3):
                large(ty, d).start()

        def arrive(d, own):
            for ty in range(2):
                if not own:
                    large(ty, d).wait_recv()
                on(ty, d).start()

        def finish():
            for ty in range(2):
                for d in range(1, 4):
                    large(ty, d).wait_send()
                for d in range(4):
                    on(ty, d).wait_send()

        return first, second, arrive, on, finish

    def score(t, ty, i):
        s = lax.dot_general(
            cbuf[t, ty, i].reshape(2 * SHARE, D), rows[t], (((1,), (1,)), ((), ())), preferred_element_type=F32)
        m = jnp.max(s, axis=0, keepdims=True)
        p = jnp.exp(s - m)
        mst[pl.ds(ty * 4 + i, 1), :] = m
        lst[pl.ds(ty * 4 + i, 1), :] = jnp.sum(p, axis=0, keepdims=True)
        pbuf[ty, i] = p.astype(BF16).reshape(2, SHARE, ROWS)

    def near_first(j):
        return j + j // 2 - 2 * (j // 3)

    def normalise(t):
        m = mst[...]
        top = jnp.max(m, axis=0, keepdims=True)
        stats[t, z, 0:1, :] = top
        stats[t, z, 1:2, :] = jnp.sum(lst[...] * jnp.exp(m - top), axis=0, keepdims=True)
        around = [send(stats.at[t, z], stats.at[t, z], zpeer(d)) for d in (4, 3, 5, 2, 6, 1, 7)]
        for c in around:
            c.wait_recv()
        peak = stats[t, 0, 0:1, :]
        for i in range(1, NZ):
            peak = jnp.maximum(peak, stats[t, i, 0:1, :])
        total = jnp.zeros_like(peak)
        for i in range(NZ):
            total = total + stats[t, i, 1:2, :] * jnp.exp(stats[t, i, 0:1, :] - peak)
        mst[...] = jnp.exp(m - peak) / total

    def reduce_sums(t, midway):
        to_core = take(8)
        to_plane = take(6)

        def core_copy(ty, i, j):
            return copy(sums.at[ty, i, 1 - k], crecv.at[t, ty, i], other, to_core + ty * 4 + j)

        def plane_copy(ty, i, d):
            return copy(abuf.at[t, ty, i], arecv.at[t, ty, d - 1], peer[ty](d), to_plane + ty * 3 + d - 1)

        def far_first(j):
            return (2 + j * (j + 1) // 2) % 4

        def combine(j):
            d = far_first(j)
            for ty in range(2):
                i = (me[ty] + d) % 4
                core_copy(ty, i, j).wait_recv()
                whole = sums[ty, i, k] + crecv[t, ty, i]
                sums[ty, i, k] = whole
                abuf[t, ty, i] = whole.astype(BF16)

                @pl.when(j < 3)
                def _():
                    plane_copy(ty, i, d).start()

        def body(j, _):
            d = far_first(j)
            for ty in range(2):
                i = (me[ty] + d) % 4
                f = mst[pl.ds(ty * 4 + i, 1), :]
                for h in range(2):
                    resp = (pbuf[ty, i, h].astype(F32) * f).astype(BF16)
                    pbuf[ty, i, h] = resp
                    wide = resp.astype(F32)
                    acc = wide[:, :128]
                    for n in range(1, ROWS // 128):
                        acc = acc + wide[:, n * 128:(n + 1) * 128]
                    gbuf[ty, i, h] = jnp.broadcast_to(jnp.sum(acc.T, axis=0, keepdims=True), (8, SHARE))
                both = jnp.dot(pbuf[ty, i].reshape(2 * SHARE, ROWS), rows[t], preferred_element_type=F32)
                sums[ty, i] = both.reshape(2, SHARE, D)
                core_copy(ty, i, j).start()

            @pl.when(j > 0)
            def _():
                combine(j - 1)

            return 0

        lax.fori_loop(0, 4, body, 0)
        for h in range(2):
            for b in range(NX):
                for q in range(NY):
                    glin[t, h, b, :, q * QUART:q * QUART + ITEM] = gbuf[0, b, h, :, q * ITEM:(q + 1) * ITEM]
                    glin[t, h, b, :, q * QUART + ITEM:(q + 1) * QUART] = gbuf[1, q, h, :, b * ITEM:(b + 1) * ITEM]
        g_core = send(glin.at[t, 1 - k], grecv.at[t], other)
        combine(3)
        midway(0)
        g_core.wait_recv()
        for c in range(NX):
            gsum[t, c] = glin[t, k, c] + grecv[t, c]
        g_x = [send(gsum.at[t, (x + d) % NX], g1recv.at[t, d - 1], xpeer(d)) for d in range(1, NX)]

        second = []
        for ty in range(2):
            for d in range(1, 4):
                plane_copy(ty, (me[ty] + d) % 4, d).wait()
            part = sums[ty, me[ty], k]
            for n in range(3):
                part = part + arecv[t, ty, n].astype(F32)
            a2f[ty] = part.reshape(4, ITEM, D)
            a2[t, ty] = part.astype(BF16).reshape(4, ITEM, D)
            second.append([
                send(a2.at[t, ty, (me[1 - ty] + d) % 4], a2recv.at[t, ty, d - 1], peer[1 - ty](d)) for d in (2, 1, 3)])
        midway(1)
        for c in g_x:
            c.wait_recv()
        g = gsum[t, x]
        for n in range(NX - 1):
            g = g + g1recv[t, n]
        g2[t] = g
        g_y = [send(g2.at[t], g2recv.at[t, d - 1], ypeer(d)) for d in range(1, NY)]
        quarter = []
        for ty in range(2):
            for c in second[ty]:
                c.wait_recv()
            whole = a2f[ty, me[1 - ty]]
            for n in range(3):
                whole = whole + a2recv[t, ty, n].astype(F32)
            quarter.append(whole)
        for c in g_y:
            c.wait_recv()
        for n in range(NY - 1):
            g = g + g2recv[t, n]
        for j in range(4):
            for ty in range(2):
                core_copy(ty, (me[ty] + far_first(j)) % 4, j).wait_send()
        return jnp.concatenate(quarter, axis=0), g

    place = pl.ds(pl.multiple_of(k * PART + y * QUART, QUART), QUART)
    lane = lax.broadcasted_iota(jnp.int32, (QUART, PART), 1)
    line = lax.broadcasted_iota(jnp.int32, (QUART, PART), 0) + y * QUART
    hit = lane == line

    def column(v):
        return jnp.sum(jnp.where(hit, v[0:1, :], 0.0), axis=1, keepdims=True)

    def update(old, mass, total, g):
        m = column(mass)
        return (m * old + total) / (m + column(g))

    hop, finish = ring(0)
    hop2, finish2 = ring(1)
    first, second, arrive, on, finish_spread = spread(0)
    hop(1)
    first(1)
    second(0, wait=False)
    hop(2)
    second(1)
    hop(3)
    arrive(0, True)
    hop(4)
    for d in (1, 3, 2):
        arrive(d, False)
    finish()

    def early(j, _):
        d = near_first(j)
        for ty in range(2):
            on(ty, d).wait_recv()
            score(0, ty, (me[ty] + 4 - d) % 4)
        return 0

    lax.fori_loop(0, 4, early, 0)
    finish_spread()
    normalise(0)
    hop2(1)
    total, g = reduce_sums(0, lambda n: hop2(2 + n))
    mass = jnp.broadcast_to(counts[pl.ds(k, 1), :], (8, PART))
    fresh = update(cents[place, :], mass, total, g)
    cur[...] = fresh
    massbuf[0, k] = mass + g
    fresh = (fresh * SHARP).astype(BF16)
    cbuf[1, 0, x, k, items(y), :] = fresh[:ITEM]
    cbuf[1, 1, y, k, items(x), :] = fresh[ITEM:]
    first, second, arrive, on, finish_spread = spread(1)
    first(0)
    first(1)
    hop2(4)
    second(0)
    second(1)
    finish2()

    def late(j, _):
        d = near_first(j)

        @pl.when(j == 0)
        def _():
            arrive(d, True)

        @pl.when((j > 0) & (j < 4))
        def _():
            arrive(d, False)

        @pl.when(j > 0)
        def _():
            before = near_first(j - 1)
            for ty in range(2):
                on(ty, before).wait_recv()
                score(1, ty, (me[ty] + 4 - before) % 4)

        return 0

    lax.fori_loop(0, 5, late, 0)
    finish_spread()
    normalise(1)
    total, g = reduce_sums(1, lambda n: None)
    mass = massbuf[0, k]
    out[place, :] = update(cur[...], mass, total, g).astype(BF16)
    around = [send(out.at[place], out.at[place], ypeer(d)) for d in (2, 1, 3)]
    passed = [send(out.at[place], out.at[place], other)]
    massbuf[1, k] = mass + g
    passed.append(send(massbuf.at[1, k], massbuf.at[1, k], other))
    for n, d in ((1, 1), (2, 3), (0, 2)):
        around[n].wait_recv()
        src = out.at[pl.ds(pl.multiple_of(k * PART + ((y + NY - d) % NY) * QUART, QUART), QUART)]
        passed.append(send(src, src, other))
    for c in passed:
        c.wait_recv()
    new_counts[0:1, :] = massbuf[1, 0, 0:1, :]
    new_counts[1:2, :] = massbuf[1, 1, 0:1, :]
    for c in sent:
        c.wait_send()
    assert used[0] <= SEMS, used[0]


def body(batch, centroids, counts):
    vmem = pl.BlockSpec(memory_space=pltpu.VMEM)
    refined, mass = pl.pallas_call(
        kernel,
        out_shape=(
            jax.ShapeDtypeStruct((BLOCK, D), BF16),
            jax.ShapeDtypeStruct((2, PART), F32),
        ),
        in_specs=[vmem] * 3,
        out_specs=(vmem, vmem),
        scratch_shapes=[
            pltpu.VMEM((2, ROWS, D), BF16),
            pltpu.VMEM((2, 2, 4, 2, SHARE, D), BF16),
            pltpu.VMEM((2, 4, 2, SHARE, ROWS), BF16),
            pltpu.VMEM((8, ROWS), F32),
            pltpu.VMEM((8, ROWS), F32),
            pltpu.VMEM((2, NZ, 2, ROWS), F32),
            pltpu.VMEM((2, 4, 2, SHARE, D), F32),
            pltpu.VMEM((2, 2, 4, SHARE, D), F32),
            pltpu.VMEM((2, 2, 4, SHARE, D), BF16),
            pltpu.VMEM((2, 2, 3, SHARE, D), BF16),
            pltpu.VMEM((2, 2, 4, ITEM, D), BF16),
            pltpu.VMEM((2, 4, ITEM, D), F32),
            pltpu.VMEM((2, 2, 3, ITEM, D), BF16),
            pltpu.VMEM((2, 4, 2, 8, SHARE), F32),
            pltpu.VMEM((2, 2, NX, 8, PART), F32),
            pltpu.VMEM((2, NX, 8, PART), F32),
            pltpu.VMEM((2, NX, 8, PART), F32),
            pltpu.VMEM((2, NX - 1, 8, PART), F32),
            pltpu.VMEM((2, 8, PART), F32),
            pltpu.VMEM((2, NY - 1, 8, PART), F32),
            pltpu.VMEM((QUART, D), F32),
            pltpu.VMEM((2, 2, 8, PART), F32),
            pltpu.SemaphoreType.DMA((SEMS,)),
            pltpu.SemaphoreType.DMA((SEMS,)),
        ],
        compiler_params=pltpu.CompilerParams(
            collective_id=0, has_side_effects=True, vmem_limit_bytes=58 * 1024 * 1024
        ),
    )(batch, centroids, counts.reshape(2, PART))
    return refined.astype(F32), mass.reshape(BLOCK)


def solution(mesh):
    return jax.shard_map(
        body,
        mesh=mesh,
        in_specs=(P(None, ("dp", "cent"), None), P("cent", None), P("cent")),
        out_specs=(P("cent", None), P("cent")),
        check_vma=False,
    )
```

```python
import jax
import jax.numpy as jnp
from jax import lax
from jax.experimental import pallas as pl
from jax.experimental.pallas import tpu as pltpu
from jax.sharding import PartitionSpec as P

MESH = pl.DeviceIdType.MESH
F32 = jnp.float32
BF16 = jnp.bfloat16
SHARP = 4.0

NX, NY, NZ = 4, 4, 8
OWN = 128
ROWS = NZ * OWN
D = 768
BLOCK = 512
PART = BLOCK // 2
QUART = PART // NY
ITEM = QUART // 2
SHARE = 4 * ITEM
SEMS = 192
OWNERS = (-1, 1, -2, 2, -3, 3, 0, 4)


def kernel(batch, cents, counts, out, new_counts, rows, cbuf, pbuf, mst, lst, stats, joint, sums, crecv, abuf, arecv,
           a2, a2f, a2recv, gbuf, glin, grecv, gsum, g1recv, g2, g2recv, cur, massbuf, send_sem, recv_sem):
    dp = lax.axis_index("dp")
    ce = lax.axis_index("cent")
    y, k = dp // 2, dp % 2
    x, z = ce // NZ, ce % NZ
    me = (x, y)

    def at(px, py, pz, pk):
        return (py * 2 + pk, px * NZ + pz)

    other = at(x, y, z, 1 - k)

    def xpeer(d):
        return at((x + d) % NX, y, z, k)

    def ypeer(d):
        return at(x, (y + d) % NY, z, k)

    def zpeer(d):
        return at(x, y, (z + d) % NZ, k)

    peer = (xpeer, ypeer)
    used = [0]
    sent = []

    def take(n=1):
        used[0] += n
        return used[0] - n

    def copy(src, dst, to, sem):
        return pltpu.make_async_remote_copy(
            src_ref=src, dst_ref=dst, send_sem=send_sem.at[sem], recv_sem=recv_sem.at[sem],
            device_id=to, device_id_type=MESH)

    def send(src, dst, to):
        c = copy(src, dst, to, take())
        c.start()
        sent.append(c)
        return c

    def items(i):
        return pl.ds(pl.multiple_of(i * ITEM, ITEM), ITEM)

    barrier = pltpu.get_barrier_semaphore()
    peers = [other]
    peers += [xpeer(d) for d in range(1, NX)]
    peers += [ypeer(d) for d in range(1, NY)]
    peers += [zpeer(d) for d in range(1, NZ)]
    for p in peers:
        pl.semaphore_signal(barrier, inc=1, device_id=p, device_id_type=MESH)

    def slot(h, sign):
        return {0: 6, 4: 7}.get(h, 2 * h - 2 + (sign < 0)) * OWN

    for t in range(2):
        rows[t, slot(0, 1):slot(0, 1) + OWN, :] = batch[t]

    def from_block(first):
        return (cents[pl.ds(pl.multiple_of(k * PART + first, ITEM), ITEM), :] * SHARP).astype(BF16)

    for q in range(NY):
        cbuf[0, 0, x, k, q * ITEM:(q + 1) * ITEM, :] = from_block(q * QUART)
    cbuf[0, 1, y, k, items(x), :] = from_block(y * QUART + ITEM)

    pl.semaphore_wait(barrier, len(peers))

    def ring(t):
        arrived = {}

        def hop(h):
            for c in (0, 1):
                for sign in (1, -1):
                    if h == 4 and c != (sign < 0):
                        continue
                    if h > 1:
                        arrived.pop((h - 1, sign, c)).wait_recv()
                    src = pl.ds(slot(h - 1, sign) + c * (OWN // 2), OWN // 2)
                    dst = pl.ds(slot(h, sign) + c * (OWN // 2), OWN // 2)
                    arrived[(h, sign, c)] = send(rows.at[t, src], rows.at[t, dst], zpeer(sign % NZ))

        def finish(last=4):
            for key in sorted(arrived):
                if key[0] <= last:
                    arrived.pop(key).wait_recv()

        return hop, finish

    def spread(t):
        near_sem = take(6)
        far_sem = take(24)
        over = take(8)

        def near(ty, n):
            src = cbuf.at[t, ty, me[ty], k, items(me[1 - ty])]
            return copy(src, src, peer[1 - ty](n), near_sem + ty * 3 + n - 1)

        def far(ty, n, d, start=True):
            block = me[ty] if start else (me[ty] + 4 - d) % 4
            src = cbuf.at[t, ty, block, k, items((me[1 - ty] + 4 - n) % 4)]
            return copy(src, src, peer[ty](d), far_sem + ty * 12 + (d - 1) * 4 + n)

        def on(ty, d):
            src = cbuf.at[t, ty, (me[ty] + 4 - d) % 4, k]
            return copy(src, src, other, over + ty * 4 + d)

        def begin(types):
            for ty in types:
                for n in (2, 1, 3):
                    near(ty, n).start()
            for ty in range(2):
                for d in (2, 1, 3):
                    far(ty, 0, d).start()

        def go_on(types):
            for n in (1, 3, 2):
                for ty in types:
                    near(ty, n).wait()
            for d in (1, 3, 2):
                for n in (1, 3, 2):
                    for ty in range(2):
                        far(ty, n, d).start()

        def arrive(d, own):
            for ty in range(2):
                if not own:
                    for n in range(4):
                        far(ty, n, d, False).wait_recv()
                on(ty, d).start()

        def finish():
            for ty in range(2):
                for d in range(1, 4):
                    for n in range(4):
                        far(ty, n, d).wait_send()
                for d in range(4):
                    on(ty, d).wait_send()

        return begin, go_on, arrive, on, finish

    def score(t, ty, i, first, size):
        s = lax.dot_general(
            cbuf[t, ty, i].reshape(2 * SHARE, D), rows[t, first:first + size, :], (((1,), (1,)), ((), ())),
            preferred_element_type=F32)
        m = jnp.max(s, axis=0, keepdims=True)
        p = jnp.exp(s - m)
        mst[pl.ds(ty * 4 + i, 1), first:first + size] = m
        lst[pl.ds(ty * 4 + i, 1), first:first + size] = jnp.sum(p, axis=0, keepdims=True)
        pbuf[ty, i, :, :, first:first + size] = p.astype(BF16).reshape(2, SHARE, size)

    def near_first(j):
        return j + j // 2 - 2 * (j // 3)

    def normalise(t):
        m = mst[...]
        top = jnp.max(m, axis=0, keepdims=True)
        low = jnp.sum(lst[...] * jnp.exp(m - top), axis=0, keepdims=True)
        places = [pl.ds(pl.multiple_of((z + NZ + off) % NZ * OWN, OWN), OWN) for off in OWNERS]
        for b, where in enumerate(places):
            stats[t, z, 0:1, where] = top[:, b * OWN:(b + 1) * OWN]
            stats[t, z, 1:2, where] = low[:, b * OWN:(b + 1) * OWN]
        around = [send(stats.at[t, z], stats.at[t, z], zpeer(d)) for d in (4, 3, 5, 2, 6, 1, 7)]
        for c in around:
            c.wait_recv()
        peak = stats[t, 0, 0:1, :]
        for i in range(1, NZ):
            peak = jnp.maximum(peak, stats[t, i, 0:1, :])
        total = jnp.zeros_like(peak)
        for i in range(NZ):
            total = total + stats[t, i, 1:2, :] * jnp.exp(stats[t, i, 0:1, :] - peak)
        joint[0:1, :] = peak
        joint[1:2, :] = total
        for b, where in enumerate(places):
            joint[2:4, b * OWN:(b + 1) * OWN] = joint[0:2, where]
        mst[...] = jnp.exp(m - joint[2:3, :]) / joint[3:4, :]

    def reduce_sums(t, midway):
        to_core = take(8)
        to_plane = take(6)

        def core_copy(ty, j):
            i = target(ty, j)
            return copy(sums.at[ty, i, 1 - k], crecv.at[t, ty, i], other, to_core + ty * 4 + j)

        def plane_copy(ty, d):
            i = (x + ty * (y - x) + d) % 4
            to = at(x + (1 - ty) * (i - x), y + ty * (i - y), z, k)
            return copy(abuf.at[t, ty, i], arecv.at[t, ty, d - 1], to, to_plane + ty * 3 + d - 1)

        def far_first(j):
            return (2 + j * (j + 1) // 2) % 4

        def target(ty, j):
            return (x + ty * (y - x) + far_first(j)) % 4

        def combine(n):
            ty, j = n % 2, n // 2
            i = target(ty, j)
            core_copy(ty, j).wait_recv()
            whole = sums[ty, i, k] + crecv[t, ty, i]
            sums[ty, i, k] = whole
            abuf[t, ty, i] = whole.astype(BF16)

            @pl.when(j < 3)
            def _():
                plane_copy(ty, far_first(j)).start()

        def body(n, _):
            ty, j = n % 2, n // 2
            i = target(ty, j)
            f = mst[pl.ds(ty * 4 + i, 1), :]
            for h in range(2):
                pbuf[ty, i, h] = (pbuf[ty, i, h].astype(F32) * f).astype(BF16)
            both = jnp.dot(pbuf[ty, i].reshape(2 * SHARE, ROWS), rows[t], preferred_element_type=F32)
            sums[ty, i] = both.reshape(2, SHARE, D)
            core_copy(ty, j).start()

            @pl.when(n > 1)
            def _():
                combine(n - 2)

            return 0

        lax.fori_loop(0, 8, body, 0)
        combine(6)
        combine(7)

        def masses(n, _):
            ty, i = n // 4, n % 4
            for h in range(2):
                wide = pbuf[ty, i, h].astype(F32)
                acc = wide[:, :128]
                for b in range(1, ROWS // 128):
                    acc = acc + wide[:, b * 128:(b + 1) * 128]
                gbuf[ty, i, h] = jnp.broadcast_to(jnp.sum(acc.T, axis=0, keepdims=True), (8, SHARE))
            return 0

        lax.fori_loop(0, 8, masses, 0)
        for h in range(2):
            for b in range(NX):
                for q in range(NY):
                    glin[t, h, b, :, q * QUART:q * QUART + ITEM] = gbuf[0, b, h, :, q * ITEM:(q + 1) * ITEM]
                    glin[t, h, b, :, q * QUART + ITEM:(q + 1) * QUART] = gbuf[1, q, h, :, b * ITEM:(b + 1) * ITEM]
        g_core = send(glin.at[t, 1 - k], grecv.at[t], other)
        midway()
        g_core.wait_recv()
        for c in range(NX):
            gsum[t, c] = glin[t, k, c] + grecv[t, c]
        g_x = [send(gsum.at[t, (x + d) % NX], g1recv.at[t, d - 1], xpeer(d)) for d in range(1, NX)]

        second = []
        for ty in range(2):
            for d in range(1, 4):
                plane_copy(ty, d).wait()
            part = sums[ty, me[ty], k]
            for n in range(3):
                part = part + arecv[t, ty, n].astype(F32)
            a2f[ty] = part.reshape(4, ITEM, D)
            a2[t, ty] = part.astype(BF16).reshape(4, ITEM, D)
            second.append([
                send(a2.at[t, ty, (me[1 - ty] + d) % 4], a2recv.at[t, ty, d - 1], peer[1 - ty](d)) for d in (2, 1, 3)])
        for c in g_x:
            c.wait_recv()
        g = gsum[t, x]
        for n in range(NX - 1):
            g = g + g1recv[t, n]
        g2[t] = g
        g_y = [send(g2.at[t], g2recv.at[t, d - 1], ypeer(d)) for d in range(1, NY)]
        quarter = []
        for ty in range(2):
            for c in second[ty]:
                c.wait_recv()
            whole = a2f[ty, me[1 - ty]]
            for n in range(3):
                whole = whole + a2recv[t, ty, n].astype(F32)
            quarter.append(whole)
        for c in g_y:
            c.wait_recv()
        for n in range(NY - 1):
            g = g + g2recv[t, n]
        for j in range(4):
            for ty in range(2):
                core_copy(ty, j).wait_send()
        return jnp.concatenate(quarter, axis=0), g

    place = pl.ds(pl.multiple_of(k * PART + y * QUART, QUART), QUART)
    lane = lax.broadcasted_iota(jnp.int32, (QUART, PART), 1)
    line = lax.broadcasted_iota(jnp.int32, (QUART, PART), 0) + y * QUART
    hit = lane == line

    def column(v):
        return jnp.sum(jnp.where(hit, v[0:1, :], 0.0), axis=1, keepdims=True)

    def update(old, mass, total, g):
        m = column(mass)
        return (m * old + total) / (m + column(g))

    hop, finish = ring(0)
    hop2, finish2 = ring(1)
    begin, go_on, arrive, on, finish_spread = spread(0)
    hop(1)
    begin((1,))
    go_on((1,))
    arrive(0, True)
    hop(2)
    arrive(1, False)
    arrive(3, False)
    hop(3)
    arrive(2, False)
    hop(4)

    def early(b):
        first, size = b * 2 * OWN, 2 * OWN

        def some(ty, _):
            s = lax.dot_general(
                cbuf[0, ty].reshape(8 * SHARE, D), rows[0, first:first + size, :], (((1,), (1,)), ((), ())),
                preferred_element_type=F32)
            for i in range(4):
                part = s[i * 2 * SHARE:(i + 1) * 2 * SHARE]
                m = jnp.max(part, axis=0, keepdims=True)
                p = jnp.exp(part - m)
                mst[pl.ds(ty * 4 + i, 1), first:first + size] = m
                lst[pl.ds(ty * 4 + i, 1), first:first + size] = jnp.sum(p, axis=0, keepdims=True)
                pbuf[ty, i, :, :, first:first + size] = p.astype(BF16).reshape(2, SHARE, size)
            return 0

        lax.fori_loop(0, 2, some, 0)

    for d in (0, 1, 3, 2):
        for ty in range(2):
            on(ty, d).wait_recv()
    early(0)
    early(1)
    finish(3)
    early(2)
    finish()
    early(3)
    finish_spread()
    normalise(0)
    hop2(1)
    total, g = reduce_sums(0, lambda: hop2(2))
    mass = jnp.broadcast_to(counts[pl.ds(pl.multiple_of(k * PART, PART), PART)].reshape(1, PART), (8, PART))
    fresh = update(cents[place, :], mass, total, g)
    cur[...] = fresh
    massbuf[0, k] = mass + g
    fresh = (fresh * SHARP).astype(BF16)
    cbuf[1, 0, x, k, items(y), :] = fresh[:ITEM]
    cbuf[1, 1, y, k, items(x), :] = fresh[ITEM:]
    begin, go_on, arrive, on, finish_spread = spread(1)
    begin((0, 1))
    hop2(3)
    go_on((0, 1))
    hop2(4)
    finish2()

    def late(j, _):
        d = near_first(j)

        @pl.when(j == 0)
        def _():
            arrive(d, True)

        @pl.when((j > 0) & (j < 4))
        def _():
            arrive(d, False)

        @pl.when(j > 0)
        def _():
            before = near_first(j - 1)
            for ty in range(2):
                on(ty, before).wait_recv()
                score(1, ty, (me[ty] + 4 - before) % 4, 0, ROWS)

        return 0

    lax.fori_loop(0, 5, late, 0)
    finish_spread()
    normalise(1)
    total, g = reduce_sums(1, lambda: None)
    mass = massbuf[0, k]
    out[place, :] = update(cur[...], mass, total, g).astype(BF16)
    around = [send(out.at[place], out.at[place], ypeer(d)) for d in (2, 1, 3)]
    passed = [send(out.at[place], out.at[place], other)]
    massbuf[1, k] = mass + g
    passed.append(send(massbuf.at[1, k], massbuf.at[1, k], other))
    for n, d in ((1, 1), (2, 3), (0, 2)):
        around[n].wait_recv()
        src = out.at[pl.ds(pl.multiple_of(k * PART + ((y + NY - d) % NY) * QUART, QUART), QUART)]
        passed.append(send(src, src, other))
    for c in passed:
        c.wait_recv()
    for h in range(2):
        new_counts[h * PART:(h + 1) * PART] = massbuf[1, h][0]
    for c in sent:
        c.wait_send()
    assert used[0] <= SEMS, used[0]


def body(batch, centroids, counts):
    vmem = pl.BlockSpec(memory_space=pltpu.VMEM)
    refined, mass = pl.pallas_call(
        kernel,
        out_shape=(
            jax.ShapeDtypeStruct((BLOCK, D), BF16),
            jax.ShapeDtypeStruct((BLOCK,), F32),
        ),
        in_specs=[vmem] * 3,
        out_specs=(vmem, vmem),
        scratch_shapes=[
            pltpu.VMEM((2, ROWS, D), BF16),
            pltpu.VMEM((2, 2, 4, 2, SHARE, D), BF16),
            pltpu.VMEM((2, 4, 2, SHARE, ROWS), BF16),
            pltpu.VMEM((8, ROWS), F32),
            pltpu.VMEM((8, ROWS), F32),
            pltpu.VMEM((2, NZ, 2, ROWS), F32),
            pltpu.VMEM((4, ROWS), F32),
            pltpu.VMEM((2, 4, 2, SHARE, D), F32),
            pltpu.VMEM((2, 2, 4, SHARE, D), F32),
            pltpu.VMEM((2, 2, 4, SHARE, D), BF16),
            pltpu.VMEM((2, 2, 3, SHARE, D), BF16),
            pltpu.VMEM((2, 2, 4, ITEM, D), BF16),
            pltpu.VMEM((2, 4, ITEM, D), F32),
            pltpu.VMEM((2, 2, 3, ITEM, D), BF16),
            pltpu.VMEM((2, 4, 2, 8, SHARE), F32),
            pltpu.VMEM((2, 2, NX, 8, PART), F32),
            pltpu.VMEM((2, NX, 8, PART), F32),
            pltpu.VMEM((2, NX, 8, PART), F32),
            pltpu.VMEM((2, NX - 1, 8, PART), F32),
            pltpu.VMEM((2, 8, PART), F32),
            pltpu.VMEM((2, NY - 1, 8, PART), F32),
            pltpu.VMEM((QUART, D), F32),
            pltpu.VMEM((2, 2, 8, PART), F32),
            pltpu.SemaphoreType.DMA((SEMS,)),
            pltpu.SemaphoreType.DMA((SEMS,)),
        ],
        compiler_params=pltpu.CompilerParams(
            collective_id=0, has_side_effects=True, vmem_limit_bytes=44 * 1024 * 1024
        ),
    )(batch, centroids, counts)
    return refined.astype(F32), mass


def solution(mesh):
    return jax.shard_map(
        body,
        mesh=mesh,
        in_specs=(P(None, ("dp", "cent"), None), P("cent", None), P("cent")),
        out_specs=(P("cent", None), P("cent")),
        check_vma=False,
    )
```

```python
import jax
import jax.numpy as jnp
from jax import lax
from jax.experimental import pallas as pl
from jax.experimental.pallas import tpu as pltpu
from jax.sharding import PartitionSpec as P

MESH = pl.DeviceIdType.MESH
F32 = jnp.float32
BF16 = jnp.bfloat16
SHARP = 4.0

NX, NY, NZ = 4, 4, 8
OWN = 128
ROWS = NZ * OWN
D = 768
BLOCK = 512
PART = BLOCK // 2
QUART = PART // NY
ITEM = QUART // 2
SHARE = 4 * ITEM
SENDS, RECVS = 20, 80
OWNERS = (-1, 1, -2, 2, -3, 3, 0, 4)


def kernel(batch, cents, counts, out, new_counts, rows, cbuf, pbuf, mst, lst, stats, joint, sums, crecv, abuf, arecv,
           a2, a2f, a2recv, gbuf, glin, grecv, gsum, g1recv, g2, g2recv, cur, massbuf, send_sem, recv_sem):
    dp = lax.axis_index("dp")
    ce = lax.axis_index("cent")
    y, k = dp // 2, dp % 2
    x, z = ce // NZ, ce % NZ
    me = (x, y)

    def at(px, py, pz, pk):
        return (py * 2 + pk, px * NZ + pz)

    other = at(x, y, z, 1 - k)

    def xpeer(d):
        return at((x + d) % NX, y, z, k)

    def ypeer(d):
        return at(x, (y + d) % NY, z, k)

    def zpeer(d):
        return at(x, y, (z + d) % NZ, k)

    peer = (xpeer, ypeer)
    used = [0, 0]

    def take(n):
        used[1] += n
        return used[1] - n

    def sender():
        used[0] += 1
        return used[0] - 1

    def copy(src, dst, to, group, sem):
        return pltpu.make_async_remote_copy(
            src_ref=src, dst_ref=dst, send_sem=send_sem.at[group], recv_sem=recv_sem.at[sem],
            device_id=to, device_id_type=MESH)

    def wait_sent(size, group):
        copy(size, size, other, group, 0).wait_send()

    def wait_arrived(size, sem):
        copy(size, size, other, 0, sem).wait_recv()

    def lines(n):
        return rows.at[0, pl.ds(0, n)]

    def items(i):
        return pl.ds(pl.multiple_of(i * ITEM, ITEM), ITEM)

    barrier = pltpu.get_barrier_semaphore()
    peers = [other]
    peers += [xpeer(d) for d in range(1, NX)]
    peers += [ypeer(d) for d in range(1, NY)]
    peers += [zpeer(d) for d in range(1, NZ)]
    for p in peers:
        pl.semaphore_signal(barrier, inc=1, device_id=p, device_id_type=MESH)

    def slot(h, sign):
        return {0: 6, 4: 7}.get(h, 2 * h - 2 + (sign < 0)) * OWN

    for t in range(2):
        rows[t, slot(0, 1):slot(0, 1) + OWN, :] = batch[t]

    def from_block(first):
        return (cents[pl.ds(pl.multiple_of(k * PART + first, ITEM), ITEM), :] * SHARP).astype(BF16)

    for q in range(NY):
        cbuf[0, 0, x, k, q * ITEM:(q + 1) * ITEM, :] = from_block(q * QUART)
    cbuf[0, 1, y, k, items(x), :] = from_block(y * QUART + ITEM)

    pl.semaphore_wait(barrier, len(peers))

    ring_from, ring_sem = sender(), take(28)

    def ring(t, parts):
        size = OWN // parts
        arrived = {}
        count = [0]

        def hop(h):
            for c in range(parts):
                for sign in (1, -1):
                    if h == 4 and (c >= parts // 2) != (sign < 0):
                        continue
                    if h > 1:
                        arrived.pop((h - 1, c, sign)).wait_recv()
                    src = pl.ds(slot(h - 1, sign) + c * size, size)
                    dst = pl.ds(slot(h, sign) + c * size, size)
                    going = copy(rows.at[t, src], rows.at[t, dst], zpeer(sign % NZ), ring_from, ring_sem + count[0])
                    going.start()
                    count[0] += 1
                    arrived[(h, c, sign)] = going

        def finish(last=4):
            for key in sorted(arrived):
                if key[0] <= last:
                    arrived.pop(key).wait_recv()
            if last == 4:
                wait_sent(lines(7 * OWN), ring_from)

        return hop, finish

    near_from, far_from, over_from = sender(), sender(), sender()
    near_sem, far_sem, over_sem = take(2), take(6), take(8)

    def spread(t):
        def near(ty, n):
            src = cbuf.at[t, ty, me[ty], k, items(me[1 - ty])]
            return copy(src, src, peer[1 - ty](n), near_from, near_sem + ty)

        def far(ty, n, d):
            src = cbuf.at[t, ty, me[ty], k, items((me[1 - ty] + 4 - n) % 4)]
            return copy(src, src, peer[ty](d), far_from, far_sem + ty * 3 + d - 1)

        def on(ty, d):
            src = cbuf.at[t, ty, (me[ty] + 4 - d) % 4, k]
            return copy(src, src, other, over_from, over_sem + ty * 4 + d)

        def begin(types):
            for ty in types:
                for n in (2, 1, 3):
                    near(ty, n).start()
            for ty in range(2):
                for d in (2, 1, 3):
                    far(ty, 0, d).start()

        def go_on(types):
            for ty in types:
                wait_arrived(lines(3 * ITEM), near_sem + ty)
            for d in (1, 3, 2):
                for n in (1, 3, 2):
                    for ty in range(2):
                        far(ty, n, d).start()

        def arrive(d, own):
            for ty in range(2):
                if not own:
                    wait_arrived(lines(SHARE), far_sem + ty * 3 + d - 1)
                on(ty, d).start()

        def finish(types):
            wait_sent(lines(3 * ITEM * len(types)), near_from)
            wait_sent(lines(6 * SHARE), far_from)
            wait_sent(lines(8 * SHARE), over_from)

        return begin, go_on, arrive, on, finish

    def score(t, ty, i, first, size):
        s = lax.dot_general(
            cbuf[t, ty, i].reshape(2 * SHARE, D), rows[t, first:first + size, :], (((1,), (1,)), ((), ())),
            preferred_element_type=F32)
        m = jnp.max(s, axis=0, keepdims=True)
        p = jnp.exp(s - m)
        mst[pl.ds(ty * 4 + i, 1), first:first + size] = m
        lst[pl.ds(ty * 4 + i, 1), first:first + size] = jnp.sum(p, axis=0, keepdims=True)
        pbuf[ty, i, :, :, first:first + size] = p.astype(BF16).reshape(2, SHARE, size)

    def near_first(j):
        return j + j // 2 - 2 * (j // 3)

    def normalise(t):
        m = mst[...]
        top = jnp.max(m, axis=0, keepdims=True)
        low = jnp.sum(lst[...] * jnp.exp(m - top), axis=0, keepdims=True)
        places = [pl.ds(pl.multiple_of((z + NZ + off) % NZ * OWN, OWN), OWN) for off in OWNERS]
        for b, where in enumerate(places):
            stats[t, z, 0:1, where] = top[:, b * OWN:(b + 1) * OWN]
            stats[t, z, 1:2, where] = low[:, b * OWN:(b + 1) * OWN]
        group, sem = sender(), take(1)
        for d in (4, 3, 5, 2, 6, 1, 7):
            copy(stats.at[t, z], stats.at[t, z], zpeer(d), group, sem).start()
        wait_arrived(stats.at[t, pl.ds(0, NZ - 1)], sem)
        wait_sent(stats.at[t, pl.ds(0, NZ - 1)], group)
        peak = stats[t, 0, 0:1, :]
        for i in range(1, NZ):
            peak = jnp.maximum(peak, stats[t, i, 0:1, :])
        total = jnp.zeros_like(peak)
        for i in range(NZ):
            total = total + stats[t, i, 1:2, :] * jnp.exp(stats[t, i, 0:1, :] - peak)
        joint[0:1, :] = peak
        joint[1:2, :] = total
        for b, where in enumerate(places):
            joint[2:4, b * OWN:(b + 1) * OWN] = joint[0:2, where]
        mst[...] = jnp.exp(m - joint[2:3, :]) / joint[3:4, :]

    core_from, plane_from, second_from, mass_from = sender(), sender(), sender(), sender()
    core_sem, plane_sem, second_sem, mass_sem = take(8), take(2), take(2), take(3)

    def reduce_sums(t, midway):

        def core_copy(ty, j):
            i = target(ty, j)
            return copy(sums.at[ty, i, 1 - k], crecv.at[t, ty, i], other, core_from, core_sem + ty * 4 + j)

        def plane_copy(ty, d):
            i = (x + ty * (y - x) + d) % 4
            to = at(x + (1 - ty) * (i - x), y + ty * (i - y), z, k)
            return copy(abuf.at[t, ty, i], arecv.at[t, ty, d - 1], to, plane_from, plane_sem + ty)

        def far_first(j):
            return (2 + j * (j + 1) // 2) % 4

        def target(ty, j):
            return (x + ty * (y - x) + far_first(j)) % 4

        def combine(n):
            ty, j = n % 2, n // 2
            i = target(ty, j)
            core_copy(ty, j).wait_recv()
            whole = sums[ty, i, k] + crecv[t, ty, i]
            sums[ty, i, k] = whole
            abuf[t, ty, i] = whole.astype(BF16)

            @pl.when(j < 3)
            def _():
                plane_copy(ty, far_first(j)).start()

        def body(n, _):
            ty, j = n % 2, n // 2
            i = target(ty, j)
            f = mst[pl.ds(ty * 4 + i, 1), :]
            for h in range(2):
                pbuf[ty, i, h] = (pbuf[ty, i, h].astype(F32) * f).astype(BF16)
            both = jnp.dot(pbuf[ty, i].reshape(2 * SHARE, ROWS), rows[t], preferred_element_type=F32)
            sums[ty, i] = both.reshape(2, SHARE, D)
            core_copy(ty, j).start()

            @pl.when(n > 1)
            def _():
                combine(n - 2)

            return 0

        lax.fori_loop(0, 8, body, 0)
        combine(6)
        combine(7)

        def masses(n, _):
            ty, i = n // 4, n % 4
            for h in range(2):
                wide = pbuf[ty, i, h].astype(F32)
                acc = wide[:, :128]
                for b in range(1, ROWS // 128):
                    acc = acc + wide[:, b * 128:(b + 1) * 128]
                gbuf[ty, i, h] = jnp.broadcast_to(jnp.sum(acc.T, axis=0, keepdims=True), (8, SHARE))
            return 0

        lax.fori_loop(0, 8, masses, 0)
        for h in range(2):
            for b in range(NX):
                for q in range(NY):
                    glin[t, h, b, :, q * QUART:q * QUART + ITEM] = gbuf[0, b, h, :, q * ITEM:(q + 1) * ITEM]
                    glin[t, h, b, :, q * QUART + ITEM:(q + 1) * QUART] = gbuf[1, q, h, :, b * ITEM:(b + 1) * ITEM]
        g_core = copy(glin.at[t, 1 - k], grecv.at[t], other, mass_from, mass_sem)
        g_core.start()
        midway()
        g_core.wait()
        for c in range(NX):
            gsum[t, c] = glin[t, k, c] + grecv[t, c]
        for d in range(1, NX):
            copy(gsum.at[t, (x + d) % NX], g1recv.at[t, d - 1], xpeer(d), mass_from, mass_sem + 1).start()

        for ty in range(2):
            wait_arrived(lines(3 * SHARE), plane_sem + ty)
            part = sums[ty, me[ty], k]
            for n in range(3):
                part = part + arecv[t, ty, n].astype(F32)
            a2f[ty] = part.reshape(4, ITEM, D)
            a2[t, ty] = part.astype(BF16).reshape(4, ITEM, D)
            for d in (2, 1, 3):
                copy(a2.at[t, ty, (me[1 - ty] + d) % 4], a2recv.at[t, ty, d - 1], peer[1 - ty](d),
                     second_from, second_sem + ty).start()
        wait_arrived(g1recv.at[t], mass_sem + 1)
        wait_sent(g1recv.at[t], mass_from)
        g = gsum[t, x]
        for n in range(NX - 1):
            g = g + g1recv[t, n]
        g2[t] = g
        for d in range(1, NY):
            copy(g2.at[t], g2recv.at[t, d - 1], ypeer(d), mass_from, mass_sem + 2).start()
        quarter = []
        for ty in range(2):
            wait_arrived(lines(3 * ITEM), second_sem + ty)
            whole = a2f[ty, me[1 - ty]]
            for n in range(3):
                whole = whole + a2recv[t, ty, n].astype(F32)
            quarter.append(whole)
        wait_arrived(g2recv.at[t], mass_sem + 2)
        wait_sent(g2recv.at[t], mass_from)
        for n in range(NY - 1):
            g = g + g2recv[t, n]
        wait_sent(sums.at[0], core_from)
        wait_sent(lines(6 * SHARE), plane_from)
        wait_sent(lines(6 * ITEM), second_from)
        return jnp.concatenate(quarter, axis=0), g

    place = pl.ds(pl.multiple_of(k * PART + y * QUART, QUART), QUART)
    lane = lax.broadcasted_iota(jnp.int32, (QUART, PART), 1)
    line = lax.broadcasted_iota(jnp.int32, (QUART, PART), 0) + y * QUART
    hit = lane == line

    def column(v):
        return jnp.sum(jnp.where(hit, v[0:1, :], 0.0), axis=1, keepdims=True)

    def update(old, mass, total, g):
        m = column(mass)
        return (m * old + total) / (m + column(g))

    hop, finish = ring(0, 4)
    hop2, finish2 = ring(1, 2)
    begin, go_on, arrive, on, finish_spread = spread(0)
    hop(1)
    begin((1,))
    go_on((1,))
    arrive(0, True)
    hop(2)
    arrive(1, False)
    arrive(3, False)
    hop(3)
    arrive(2, False)
    hop(4)

    def early(b):
        first, size = b * 2 * OWN, 2 * OWN

        def some(ty, _):
            s = lax.dot_general(
                cbuf[0, ty].reshape(8 * SHARE, D), rows[0, first:first + size, :], (((1,), (1,)), ((), ())),
                preferred_element_type=F32)
            for i in range(4):
                part = s[i * 2 * SHARE:(i + 1) * 2 * SHARE]
                m = jnp.max(part, axis=0, keepdims=True)
                p = jnp.exp(part - m)
                mst[pl.ds(ty * 4 + i, 1), first:first + size] = m
                lst[pl.ds(ty * 4 + i, 1), first:first + size] = jnp.sum(p, axis=0, keepdims=True)
                pbuf[ty, i, :, :, first:first + size] = p.astype(BF16).reshape(2, SHARE, size)
            return 0

        lax.fori_loop(0, 2, some, 0)

    for d in (0, 1, 3, 2):
        for ty in range(2):
            on(ty, d).wait_recv()
    early(0)
    early(1)
    finish(3)
    early(2)
    finish()
    early(3)
    finish_spread((1,))
    normalise(0)
    hop2(1)
    total, g = reduce_sums(0, lambda: hop2(2))
    mass = jnp.broadcast_to(counts[pl.ds(pl.multiple_of(k * PART, PART), PART)].reshape(1, PART), (8, PART))
    fresh = update(cents[place, :], mass, total, g)
    cur[...] = fresh
    massbuf[0, k] = mass + g
    fresh = (fresh * SHARP).astype(BF16)
    cbuf[1, 0, x, k, items(y), :] = fresh[:ITEM]
    cbuf[1, 1, y, k, items(x), :] = fresh[ITEM:]
    begin, go_on, arrive, on, finish_spread = spread(1)
    begin((0, 1))
    hop2(3)
    go_on((0, 1))
    hop2(4)
    finish2()

    def late(j, _):
        d = near_first(j)

        @pl.when(j == 0)
        def _():
            arrive(d, True)

        @pl.when((j > 0) & (j < 4))
        def _():
            arrive(d, False)

        @pl.when(j > 0)
        def _():
            before = near_first(j - 1)
            for ty in range(2):
                on(ty, before).wait_recv()
                score(1, ty, (me[ty] + 4 - before) % 4, 0, ROWS)

        return 0

    lax.fori_loop(0, 5, late, 0)
    finish_spread((0, 1))
    normalise(1)
    total, g = reduce_sums(1, lambda: None)
    mass = massbuf[0, k]
    out[place, :] = update(cur[...], mass, total, g).astype(BF16)
    from_final, from_passed, from_mass = sender(), sender(), sender()
    final_sem, passed_sem, new_sem = take(3), take(1), take(1)

    def pass_on(d):
        src = out.at[pl.ds(pl.multiple_of(k * PART + ((y + NY - d) % NY) * QUART, QUART), QUART)]
        copy(src, src, other, from_passed, passed_sem).start()

    for d in (2, 1, 3):
        copy(out.at[place], out.at[place], ypeer(d), from_final, final_sem + d - 1).start()
    pass_on(0)
    massbuf[1, k] = mass + g
    copy(massbuf.at[1, k], massbuf.at[1, k], other, from_mass, new_sem).start()
    for d in (1, 3, 2):
        wait_arrived(out.at[place], final_sem + d - 1)
        pass_on(d)
    wait_arrived(out.at[pl.ds(0, 4 * QUART)], passed_sem)
    wait_arrived(massbuf.at[1, k], new_sem)
    for h in range(2):
        new_counts[h * PART:(h + 1) * PART] = massbuf[1, h][0]
    wait_sent(out.at[pl.ds(0, 3 * QUART)], from_final)
    wait_sent(out.at[pl.ds(0, 4 * QUART)], from_passed)
    wait_sent(massbuf.at[1, 0], from_mass)
    assert used[0] <= SENDS and used[1] <= RECVS, used


def body(batch, centroids, counts):
    vmem = pl.BlockSpec(memory_space=pltpu.VMEM)
    refined, mass = pl.pallas_call(
        kernel,
        out_shape=(
            jax.ShapeDtypeStruct((BLOCK, D), BF16),
            jax.ShapeDtypeStruct((BLOCK,), F32),
        ),
        in_specs=[vmem] * 3,
        out_specs=(vmem, vmem),
        scratch_shapes=[
            pltpu.VMEM((2, ROWS, D), BF16),
            pltpu.VMEM((2, 2, 4, 2, SHARE, D), BF16),
            pltpu.VMEM((2, 4, 2, SHARE, ROWS), BF16),
            pltpu.VMEM((8, ROWS), F32),
            pltpu.VMEM((8, ROWS), F32),
            pltpu.VMEM((2, NZ, 2, ROWS), F32),
            pltpu.VMEM((4, ROWS), F32),
            pltpu.VMEM((2, 4, 2, SHARE, D), F32),
            pltpu.VMEM((2, 2, 4, SHARE, D), F32),
            pltpu.VMEM((2, 2, 4, SHARE, D), BF16),
            pltpu.VMEM((2, 2, 3, SHARE, D), BF16),
            pltpu.VMEM((2, 2, 4, ITEM, D), BF16),
            pltpu.VMEM((2, 4, ITEM, D), F32),
            pltpu.VMEM((2, 2, 3, ITEM, D), BF16),
            pltpu.VMEM((2, 4, 2, 8, SHARE), F32),
            pltpu.VMEM((2, 2, NX, 8, PART), F32),
            pltpu.VMEM((2, NX, 8, PART), F32),
            pltpu.VMEM((2, NX, 8, PART), F32),
            pltpu.VMEM((2, NX - 1, 8, PART), F32),
            pltpu.VMEM((2, 8, PART), F32),
            pltpu.VMEM((2, NY - 1, 8, PART), F32),
            pltpu.VMEM((QUART, D), F32),
            pltpu.VMEM((2, 2, 8, PART), F32),
            pltpu.SemaphoreType.DMA((SENDS,)),
            pltpu.SemaphoreType.DMA((RECVS,)),
        ],
        compiler_params=pltpu.CompilerParams(
            collective_id=0, has_side_effects=True, vmem_limit_bytes=44 * 1024 * 1024
        ),
    )(batch, centroids, counts)
    return refined.astype(F32), mass


def solution(mesh):
    return jax.shard_map(
        body,
        mesh=mesh,
        in_specs=(P(None, ("dp", "cent"), None), P("cent", None), P("cent")),
        out_specs=(P("cent", None), P("cent")),
        check_vma=False,
    )
```

```python
import jax
import jax.numpy as jnp
from jax import lax
from jax.experimental import pallas as pl
from jax.experimental.pallas import tpu as pltpu
from jax.sharding import PartitionSpec as P

MESH = pl.DeviceIdType.MESH
F32 = jnp.float32
BF16 = jnp.bfloat16
SHARP = 4.0

NX, NY, NZ = 4, 4, 8
OWN = 128
ROWS = NZ * OWN
D = 768
BLOCK = 512
PART = BLOCK // 2
QUART = PART // NY
ITEM = QUART // 2
SHARE = 4 * ITEM
SENDS, RECVS = 20, 80
OWNERS = (-1, 1, -2, 2, -3, 3, 0, 4)


def kernel(batch, cents_hbm, counts_hbm, out, new_counts, rows, cbuf, pbuf, mst, lst, stats, joint, sums, crecv, abuf, arecv,
           a2, a2f, a2recv, gbuf, glin, grecv, gsum, g1recv, g2, g2recv, cur, massbuf, cents, counts, load_sem,
           send_sem, recv_sem):
    dp = lax.axis_index("dp")
    ce = lax.axis_index("cent")
    y, k = dp // 2, dp % 2
    x, z = ce // NZ, ce % NZ
    me = (x, y)

    def at(px, py, pz, pk):
        return (py * 2 + pk, px * NZ + pz)

    other = at(x, y, z, 1 - k)

    def xpeer(d):
        return at((x + d) % NX, y, z, k)

    def ypeer(d):
        return at(x, (y + d) % NY, z, k)

    def zpeer(d):
        return at(x, y, (z + d) % NZ, k)

    peer = (xpeer, ypeer)
    used = [0, 0]

    def take(n):
        used[1] += n
        return used[1] - n

    def sender():
        used[0] += 1
        return used[0] - 1

    def copy(src, dst, to, group, sem):
        return pltpu.make_async_remote_copy(
            src_ref=src, dst_ref=dst, send_sem=send_sem.at[group], recv_sem=recv_sem.at[sem],
            device_id=to, device_id_type=MESH)

    def wait_sent(size, group):
        copy(size, size, other, group, 0).wait_send()

    def wait_arrived(size, sem):
        copy(size, size, other, 0, sem).wait_recv()

    def lines(n):
        return rows.at[0, pl.ds(0, n)]

    def items(i):
        return pl.ds(pl.multiple_of(i * ITEM, ITEM), ITEM)

    def slot(h, sign):
        return {0: 6, 4: 7}.get(h, 2 * h - 2 + (sign < 0)) * OWN

    core_half = pl.ds(pl.multiple_of(k * PART, PART), PART)
    own_rows = pl.ds(slot(0, 1), OWN)
    loads = [
        pltpu.make_async_copy(cents_hbm.at[core_half], cents, load_sem.at[0]),
        pltpu.make_async_copy(batch.at[0], rows.at[0, own_rows], load_sem.at[1]),
        pltpu.make_async_copy(batch.at[1], rows.at[1, own_rows], load_sem.at[2]),
        pltpu.make_async_copy(counts_hbm, counts, load_sem.at[3]),
    ]
    for c in loads:
        c.start()

    barrier = pltpu.get_barrier_semaphore()
    peers = [other]
    peers += [xpeer(d) for d in range(1, NX)]
    peers += [ypeer(d) for d in range(1, NY)]
    peers += [zpeer(d) for d in (1, NZ - 1)]
    for p in peers:
        pl.semaphore_signal(barrier, inc=1, device_id=p, device_id_type=MESH)

    loads[0].wait()

    def from_block(first):
        return (cents[pl.ds(pl.multiple_of(first, ITEM), ITEM), :] * SHARP).astype(BF16)

    for q in range(NY):
        cbuf[0, 0, x, k, q * ITEM:(q + 1) * ITEM, :] = from_block(q * QUART)
    cbuf[0, 1, y, k, items(x), :] = from_block(y * QUART + ITEM)

    for c in loads[1:]:
        c.wait()
    pl.semaphore_wait(barrier, len(peers))

    ring_from, ring_sem = sender(), take(28)

    def ring(t, parts):
        size = OWN // parts
        arrived = {}
        count = [0]

        def hop(h):
            for c in range(parts):
                for sign in (1, -1):
                    if h == 4 and (c >= parts // 2) != (sign < 0):
                        continue
                    if h > 1:
                        arrived.pop((h - 1, c, sign)).wait_recv()
                    src = pl.ds(slot(h - 1, sign) + c * size, size)
                    dst = pl.ds(slot(h, sign) + c * size, size)
                    going = copy(rows.at[t, src], rows.at[t, dst], zpeer(sign % NZ), ring_from, ring_sem + count[0])
                    going.start()
                    count[0] += 1
                    arrived[(h, c, sign)] = going

        def finish(last=4):
            for key in sorted(arrived):
                if key[0] <= last:
                    arrived.pop(key).wait_recv()
            if last == 4:
                wait_sent(lines(7 * OWN), ring_from)

        return hop, finish

    near_from, far_from, over_from = sender(), sender(), sender()
    near_sem, far_sem, over_sem = take(2), take(6), take(8)

    def spread(t):
        def near(ty, n):
            src = cbuf.at[t, ty, me[ty], k, items(me[1 - ty])]
            return copy(src, src, peer[1 - ty](n), near_from, near_sem + ty)

        def far(ty, n, d):
            src = cbuf.at[t, ty, me[ty], k, items((me[1 - ty] + 4 - n) % 4)]
            return copy(src, src, peer[ty](d), far_from, far_sem + ty * 3 + d - 1)

        def on(ty, d):
            src = cbuf.at[t, ty, (me[ty] + 4 - d) % 4, k]
            return copy(src, src, other, over_from, over_sem + ty * 4 + d)

        def begin(types):
            for ty in types:
                for n in (2, 1, 3):
                    near(ty, n).start()
            for ty in range(2):
                for d in (2, 1, 3):
                    far(ty, 0, d).start()

        def go_on(types, come):
            for ty in come:
                wait_arrived(lines(3 * ITEM), near_sem + ty)
            for d in (1, 3, 2):
                for n in (1, 3, 2):
                    for ty in types:
                        far(ty, n, d).start()

        def arrive(d, own):
            for ty in range(2):
                if not own:
                    wait_arrived(lines(SHARE), far_sem + ty * 3 + d - 1)
                on(ty, d).start()

        def finish(types):
            wait_sent(lines(3 * ITEM * len(types)), near_from)
            wait_sent(lines(6 * SHARE), far_from)
            wait_sent(lines(8 * SHARE), over_from)

        return begin, go_on, arrive, on, finish

    def score(t, ty, i, first, size):
        s = lax.dot_general(
            cbuf[t, ty, i].reshape(2 * SHARE, D), rows[t, first:first + size, :], (((1,), (1,)), ((), ())),
            preferred_element_type=F32)
        m = jnp.max(s, axis=0, keepdims=True)
        p = jnp.exp(s - m)
        mst[pl.ds(ty * 4 + i, 1), first:first + size] = m
        lst[pl.ds(ty * 4 + i, 1), first:first + size] = jnp.sum(p, axis=0, keepdims=True)
        pbuf[ty, i, :, :, first:first + size] = p.astype(BF16).reshape(2, SHARE, size)

    def near_first(j):
        return j + j // 2 - 2 * (j // 3)

    def normalise(t):
        m = mst[...]
        top = jnp.max(m, axis=0, keepdims=True)
        low = jnp.sum(lst[...] * jnp.exp(m - top), axis=0, keepdims=True)
        places = [pl.ds(pl.multiple_of((z + NZ + off) % NZ * OWN, OWN), OWN) for off in OWNERS]
        for b, where in enumerate(places):
            stats[t, z, 0:1, where] = top[:, b * OWN:(b + 1) * OWN]
            stats[t, z, 1:2, where] = low[:, b * OWN:(b + 1) * OWN]
        group, sem = sender(), take(1)
        for d in (4, 3, 5, 2, 6, 1, 7):
            copy(stats.at[t, z], stats.at[t, z], zpeer(d), group, sem).start()
        wait_arrived(stats.at[t, pl.ds(0, NZ - 1)], sem)
        wait_sent(stats.at[t, pl.ds(0, NZ - 1)], group)
        peak = stats[t, 0, 0:1, :]
        for i in range(1, NZ):
            peak = jnp.maximum(peak, stats[t, i, 0:1, :])
        total = jnp.zeros_like(peak)
        for i in range(NZ):
            total = total + stats[t, i, 1:2, :] * jnp.exp(stats[t, i, 0:1, :] - peak)
        joint[0:1, :] = peak
        joint[1:2, :] = total
        for b, where in enumerate(places):
            joint[2:4, b * OWN:(b + 1) * OWN] = joint[0:2, where]
        mst[...] = jnp.exp(m - joint[2:3, :]) / joint[3:4, :]

    core_from, plane_from, second_from, mass_from = sender(), sender(), sender(), sender()
    core_sem, plane_sem, second_sem, mass_sem = take(8), take(2), take(2), take(3)

    def reduce_sums(t, midway):

        def core_copy(ty, j):
            i = target(ty, j)
            return copy(sums.at[ty, i, 1 - k], crecv.at[t, ty, i], other, core_from, core_sem + ty * 4 + j)

        def plane_copy(ty, d):
            i = (x + ty * (y - x) + d) % 4
            to = at(x + (1 - ty) * (i - x), y + ty * (i - y), z, k)
            return copy(abuf.at[t, ty, i], arecv.at[t, ty, d - 1], to, plane_from, plane_sem + ty)

        def far_first(j):
            return (2 + j * (j + 1) // 2) % 4

        def target(ty, j):
            return (x + ty * (y - x) + far_first(j)) % 4

        def combine(n):
            ty, j = n % 2, n // 2
            i = target(ty, j)
            core_copy(ty, j).wait_recv()
            whole = sums[ty, i, k] + crecv[t, ty, i]
            sums[ty, i, k] = whole
            abuf[t, ty, i] = whole.astype(BF16)

            @pl.when(j < 3)
            def _():
                plane_copy(ty, far_first(j)).start()

        def body(n, _):
            ty, j = n % 2, n // 2
            i = target(ty, j)
            f = mst[pl.ds(ty * 4 + i, 1), :]
            for h in range(2):
                pbuf[ty, i, h] = (pbuf[ty, i, h].astype(F32) * f).astype(BF16)
            both = jnp.dot(pbuf[ty, i].reshape(2 * SHARE, ROWS), rows[t], preferred_element_type=F32)
            sums[ty, i] = both.reshape(2, SHARE, D)
            core_copy(ty, j).start()

            @pl.when(n > 1)
            def _():
                combine(n - 2)

            return 0

        lax.fori_loop(0, 8, body, 0)
        combine(6)
        combine(7)

        def masses(n, _):
            ty, i = n // 4, n % 4
            for h in range(2):
                wide = pbuf[ty, i, h].astype(F32)
                acc = wide[:, :128]
                for b in range(1, ROWS // 128):
                    acc = acc + wide[:, b * 128:(b + 1) * 128]
                gbuf[ty, i, h] = jnp.broadcast_to(jnp.sum(acc.T, axis=0, keepdims=True), (8, SHARE))
            return 0

        lax.fori_loop(0, 8, masses, 0)
        for h in range(2):
            for b in range(NX):
                for q in range(NY):
                    glin[t, h, b, :, q * QUART:q * QUART + ITEM] = gbuf[0, b, h, :, q * ITEM:(q + 1) * ITEM]
                    glin[t, h, b, :, q * QUART + ITEM:(q + 1) * QUART] = gbuf[1, q, h, :, b * ITEM:(b + 1) * ITEM]
        g_core = copy(glin.at[t, 1 - k], grecv.at[t], other, mass_from, mass_sem)
        g_core.start()
        g_core.wait()
        for c in range(NX):
            gsum[t, c] = glin[t, k, c] + grecv[t, c]
        for d in range(1, NX):
            copy(gsum.at[t, (x + d) % NX], g1recv.at[t, d - 1], xpeer(d), mass_from, mass_sem + 1).start()

        for ty in range(2):
            wait_arrived(lines(3 * SHARE), plane_sem + ty)
            part = sums[ty, me[ty], k]
            for n in range(3):
                part = part + arecv[t, ty, n].astype(F32)
            a2f[ty] = part.reshape(4, ITEM, D)
            a2[t, ty] = part.astype(BF16).reshape(4, ITEM, D)
            for d in (2, 1, 3):
                copy(a2.at[t, ty, (me[1 - ty] + d) % 4], a2recv.at[t, ty, d - 1], peer[1 - ty](d),
                     second_from, second_sem + ty).start()
        midway()
        wait_arrived(g1recv.at[t], mass_sem + 1)
        wait_sent(g1recv.at[t], mass_from)
        g = gsum[t, x]
        for n in range(NX - 1):
            g = g + g1recv[t, n]
        g2[t] = g
        for d in range(1, NY):
            copy(g2.at[t], g2recv.at[t, d - 1], ypeer(d), mass_from, mass_sem + 2).start()
        quarter = []
        for ty in range(2):
            wait_arrived(lines(3 * ITEM), second_sem + ty)
            whole = a2f[ty, me[1 - ty]]
            for n in range(3):
                whole = whole + a2recv[t, ty, n].astype(F32)
            quarter.append(whole)
        wait_arrived(g2recv.at[t], mass_sem + 2)
        wait_sent(g2recv.at[t], mass_from)
        for n in range(NY - 1):
            g = g + g2recv[t, n]
        wait_sent(sums.at[0], core_from)
        wait_sent(lines(6 * SHARE), plane_from)
        wait_sent(lines(6 * ITEM), second_from)
        return jnp.concatenate(quarter, axis=0), g

    place = pl.ds(pl.multiple_of(k * PART + y * QUART, QUART), QUART)
    quarter = pl.ds(pl.multiple_of(y * QUART, QUART), QUART)
    lane = lax.broadcasted_iota(jnp.int32, (QUART, PART), 1)
    line = lax.broadcasted_iota(jnp.int32, (QUART, PART), 0) + y * QUART
    hit = lane == line

    def column(v):
        return jnp.sum(jnp.where(hit, v[0:1, :], 0.0), axis=1, keepdims=True)

    def update(old, mass, total, g):
        m = column(mass)
        return (m * old + total) / (m + column(g))

    hop, finish = ring(0, 2)
    hop2, finish2 = ring(1, 2)
    begin, go_on, arrive, on, finish_spread = spread(0)
    hop(1)
    begin((1,))
    go_on((0, 1), (1,))
    hop(2)
    arrive(0, True)
    arrive(1, False)
    arrive(3, False)
    hop(3)
    arrive(2, False)
    hop(4)

    def early(b):
        first, size = b * 2 * OWN, 2 * OWN

        def some(ty, _):
            s = lax.dot_general(
                cbuf[0, ty].reshape(8 * SHARE, D), rows[0, first:first + size, :], (((1,), (1,)), ((), ())),
                preferred_element_type=F32)
            for i in range(4):
                part = s[i * 2 * SHARE:(i + 1) * 2 * SHARE]
                m = jnp.max(part, axis=0, keepdims=True)
                p = jnp.exp(part - m)
                mst[pl.ds(ty * 4 + i, 1), first:first + size] = m
                lst[pl.ds(ty * 4 + i, 1), first:first + size] = jnp.sum(p, axis=0, keepdims=True)
                pbuf[ty, i, :, :, first:first + size] = p.astype(BF16).reshape(2, SHARE, size)
            return 0

        lax.fori_loop(0, 2, some, 0)

    for d in (0, 1, 3, 2):
        for ty in range(2):
            on(ty, d).wait_recv()
    early(0)
    early(1)
    finish(3)
    early(2)
    finish()
    early(3)
    finish_spread((1,))
    normalise(0)
    hop2(1)
    total, g = reduce_sums(0, lambda: hop2(2))
    mass = jnp.broadcast_to(counts[pl.ds(pl.multiple_of(k * PART, PART), PART)].reshape(1, PART), (8, PART))
    fresh = update(cents[quarter, :], mass, total, g)
    cur[...] = fresh
    massbuf[0, k] = mass + g
    fresh = (fresh * SHARP).astype(BF16)
    cbuf[1, 0, x, k, items(y), :] = fresh[:ITEM]
    cbuf[1, 1, y, k, items(x), :] = fresh[ITEM:]
    begin, go_on, arrive, on, finish_spread = spread(1)
    begin((0, 1))
    hop2(3)
    go_on((0, 1), (0, 1))
    hop2(4)
    finish2()

    def late(j, _):
        d = near_first(j)

        @pl.when(j == 0)
        def _():
            arrive(d, True)

        @pl.when((j > 0) & (j < 4))
        def _():
            arrive(d, False)

        @pl.when(j > 0)
        def _():
            before = near_first(j - 1)
            for ty in range(2):
                on(ty, before).wait_recv()
                score(1, ty, (me[ty] + 4 - before) % 4, 0, ROWS)

        return 0

    lax.fori_loop(0, 5, late, 0)
    finish_spread((0, 1))
    normalise(1)
    total, g = reduce_sums(1, lambda: None)
    mass = massbuf[0, k]
    out[place, :] = update(cur[...], mass, total, g).astype(BF16)
    from_final, from_passed, from_mass = sender(), sender(), sender()
    final_sem, passed_sem, new_sem = take(3), take(1), take(1)

    def pass_on(d):
        src = out.at[pl.ds(pl.multiple_of(k * PART + ((y + NY - d) % NY) * QUART, QUART), QUART)]
        copy(src, src, other, from_passed, passed_sem).start()

    for d in (2, 1, 3):
        copy(out.at[place], out.at[place], ypeer(d), from_final, final_sem + d - 1).start()
    pass_on(0)
    massbuf[1, k] = mass + g
    copy(massbuf.at[1, k], massbuf.at[1, k], other, from_mass, new_sem).start()
    for d in (1, 3, 2):
        wait_arrived(out.at[place], final_sem + d - 1)
        pass_on(d)
    wait_arrived(out.at[pl.ds(0, 4 * QUART)], passed_sem)
    wait_arrived(massbuf.at[1, k], new_sem)
    for h in range(2):
        new_counts[h * PART:(h + 1) * PART] = massbuf[1, h][0]
    wait_sent(out.at[pl.ds(0, 3 * QUART)], from_final)
    wait_sent(out.at[pl.ds(0, 4 * QUART)], from_passed)
    wait_sent(massbuf.at[1, 0], from_mass)
    assert used[0] <= SENDS and used[1] <= RECVS, used


def body(batch, centroids, counts):
    vmem = pl.BlockSpec(memory_space=pltpu.VMEM)
    refined, mass = pl.pallas_call(
        kernel,
        out_shape=(
            jax.ShapeDtypeStruct((BLOCK, D), BF16),
            jax.ShapeDtypeStruct((BLOCK,), F32),
        ),
        in_specs=[pl.BlockSpec(memory_space=pltpu.HBM)] * 3,
        out_specs=(vmem, vmem),
        scratch_shapes=[
            pltpu.VMEM((2, ROWS, D), BF16),
            pltpu.VMEM((2, 2, 4, 2, SHARE, D), BF16),
            pltpu.VMEM((2, 4, 2, SHARE, ROWS), BF16),
            pltpu.VMEM((8, ROWS), F32),
            pltpu.VMEM((8, ROWS), F32),
            pltpu.VMEM((2, NZ, 2, ROWS), F32),
            pltpu.VMEM((4, ROWS), F32),
            pltpu.VMEM((2, 4, 2, SHARE, D), F32),
            pltpu.VMEM((2, 2, 4, SHARE, D), F32),
            pltpu.VMEM((2, 2, 4, SHARE, D), BF16),
            pltpu.VMEM((2, 2, 3, SHARE, D), BF16),
            pltpu.VMEM((2, 2, 4, ITEM, D), BF16),
            pltpu.VMEM((2, 4, ITEM, D), F32),
            pltpu.VMEM((2, 2, 3, ITEM, D), BF16),
            pltpu.VMEM((2, 4, 2, 8, SHARE), F32),
            pltpu.VMEM((2, 2, NX, 8, PART), F32),
            pltpu.VMEM((2, NX, 8, PART), F32),
            pltpu.VMEM((2, NX, 8, PART), F32),
            pltpu.VMEM((2, NX - 1, 8, PART), F32),
            pltpu.VMEM((2, 8, PART), F32),
            pltpu.VMEM((2, NY - 1, 8, PART), F32),
            pltpu.VMEM((QUART, D), F32),
            pltpu.VMEM((2, 2, 8, PART), F32),
            pltpu.VMEM((PART, D), F32),
            pltpu.VMEM((BLOCK,), F32),
            pltpu.SemaphoreType.DMA((4,)),
            pltpu.SemaphoreType.DMA((SENDS,)),
            pltpu.SemaphoreType.DMA((RECVS,)),
        ],
        compiler_params=pltpu.CompilerParams(
            collective_id=0, has_side_effects=True, vmem_limit_bytes=58 * 1024 * 1024
        ),
    )(batch, centroids, counts)
    return refined.astype(F32), mass


def solution(mesh):
    return jax.shard_map(
        body,
        mesh=mesh,
        in_specs=(P(None, ("dp", "cent"), None), P("cent", None), P("cent")),
        out_specs=(P("cent", None), P("cent")),
        check_vma=False,
    )
```

```python
import jax
import jax.numpy as jnp
from jax import lax
from jax.experimental import pallas as pl
from jax.experimental.pallas import tpu as pltpu
from jax.sharding import PartitionSpec as P

MESH = pl.DeviceIdType.MESH
F32 = jnp.float32
BF16 = jnp.bfloat16
SHARP = 4.0

NX, NY, NZ = 4, 4, 8
OWN = 128
ROWS = NZ * OWN
D = 768
BLOCK = 512
PART = BLOCK // 2
QUART = PART // NY
ITEM = QUART // 2
SHARE = 4 * ITEM
SENDS, RECVS = 20, 80
OWNERS = (-1, 1, -2, 2, -3, 3, 0, 4)


def kernel(batch, cents_hbm, counts_hbm, out, new_counts, rows, cbuf, pbuf, mst, lst, stats, joint, sums, crecv, abuf, arecv, onward,
           a2, a2f, a2recv, gbuf, glin, grecv, gsum, g1recv, g2, g2recv, cur, massbuf, cents, counts, load_sem,
           send_sem, recv_sem):
    dp = lax.axis_index("dp")
    ce = lax.axis_index("cent")
    y, k = dp // 2, dp % 2
    x, z = ce // NZ, ce % NZ
    me = (x, y)

    def at(px, py, pz, pk):
        return (py * 2 + pk, px * NZ + pz)

    other = at(x, y, z, 1 - k)

    def xpeer(d):
        return at((x + d) % NX, y, z, k)

    def ypeer(d):
        return at(x, (y + d) % NY, z, k)

    def zpeer(d):
        return at(x, y, (z + d) % NZ, k)

    peer = (xpeer, ypeer)
    used = [0, 0]

    def take(n):
        used[1] += n
        return used[1] - n

    def sender():
        used[0] += 1
        return used[0] - 1

    def copy(src, dst, to, group, sem):
        return pltpu.make_async_remote_copy(
            src_ref=src, dst_ref=dst, send_sem=send_sem.at[group], recv_sem=recv_sem.at[sem],
            device_id=to, device_id_type=MESH)

    def wait_sent(size, group):
        copy(size, size, other, group, 0).wait_send()

    def wait_arrived(size, sem):
        copy(size, size, other, 0, sem).wait_recv()

    def lines(n):
        return rows.at[0, pl.ds(0, n)]

    def items(i):
        return pl.ds(pl.multiple_of(i * ITEM, ITEM), ITEM)

    def slot(h, sign):
        return {0: 6, 4: 7}.get(h, 2 * h - 2 + (sign < 0)) * OWN

    core_half = pl.ds(pl.multiple_of(k * PART, PART), PART)
    own_rows = pl.ds(slot(0, 1), OWN)
    loads = [
        pltpu.make_async_copy(cents_hbm.at[core_half], cents, load_sem.at[0]),
        pltpu.make_async_copy(batch.at[0], rows.at[0, own_rows], load_sem.at[1]),
        pltpu.make_async_copy(batch.at[1], rows.at[1, own_rows], load_sem.at[2]),
        pltpu.make_async_copy(counts_hbm, counts, load_sem.at[3]),
    ]
    for c in loads:
        c.start()

    barrier = pltpu.get_barrier_semaphore()
    peers = [other]
    peers += [xpeer(d) for d in range(1, NX)]
    peers += [ypeer(d) for d in range(1, NY)]
    peers += [zpeer(d) for d in (1, NZ - 1)]
    for p in peers:
        pl.semaphore_signal(barrier, inc=1, device_id=p, device_id_type=MESH)

    loads[0].wait()

    def from_block(first):
        return (cents[pl.ds(pl.multiple_of(first, ITEM), ITEM), :] * SHARP).astype(BF16)

    for q in range(NY):
        cbuf[0, 0, x, k, q * ITEM:(q + 1) * ITEM, :] = from_block(q * QUART)
    cbuf[0, 1, y, k, items(x), :] = from_block(y * QUART + ITEM)

    for c in loads[1:]:
        c.wait()
    pl.semaphore_wait(barrier, len(peers))

    ring_from, ring_sem = sender(), take(28)

    def ring(t, parts):
        size = OWN // parts
        arrived = {}
        count = [0]

        def hop(h):
            for c in range(parts):
                for sign in (1, -1):
                    if h == 4 and (c >= parts // 2) != (sign < 0):
                        continue
                    if h > 1:
                        arrived.pop((h - 1, c, sign)).wait_recv()
                    src = pl.ds(slot(h - 1, sign) + c * size, size)
                    dst = pl.ds(slot(h, sign) + c * size, size)
                    going = copy(rows.at[t, src], rows.at[t, dst], zpeer(sign % NZ), ring_from, ring_sem + count[0])
                    going.start()
                    count[0] += 1
                    arrived[(h, c, sign)] = going

        def finish(last=4):
            for key in sorted(arrived):
                if key[0] <= last:
                    arrived.pop(key).wait_recv()
            if last == 4:
                wait_sent(lines(7 * OWN), ring_from)

        return hop, finish

    near_from, far_from, over_from = sender(), sender(), sender()
    near_sem, far_sem, over_sem = take(2), take(6), take(8)

    def spread(t):
        def near(ty, n):
            src = cbuf.at[t, ty, me[ty], k, items(me[1 - ty])]
            return copy(src, src, peer[1 - ty](n), near_from, near_sem + ty)

        def far(ty, n, d):
            src = cbuf.at[t, ty, me[ty], k, items((me[1 - ty] + 4 - n) % 4)]
            return copy(src, src, peer[ty](d), far_from, far_sem + ty * 3 + d - 1)

        def on(ty, d):
            src = cbuf.at[t, ty, (me[ty] + 4 - d) % 4, k]
            return copy(src, src, other, over_from, over_sem + ty * 4 + d)

        def begin(types):
            for ty in types:
                for n in (2, 1, 3):
                    near(ty, n).start()
            for ty in range(2):
                for d in (2, 1, 3):
                    far(ty, 0, d).start()

        def go_on(types, come):
            for ty in come:
                wait_arrived(lines(3 * ITEM), near_sem + ty)
            for d in (1, 3, 2):
                for n in (1, 3, 2):
                    for ty in types:
                        far(ty, n, d).start()

        def arrive(d, own):
            for ty in range(2):
                if not own:
                    wait_arrived(lines(SHARE), far_sem + ty * 3 + d - 1)
                on(ty, d).start()

        def finish(types):
            wait_sent(lines(3 * ITEM * len(types)), near_from)
            wait_sent(lines(6 * SHARE), far_from)
            wait_sent(lines(8 * SHARE), over_from)

        return begin, go_on, arrive, on, finish

    def score(t, ty, i, first, size):
        s = lax.dot_general(
            cbuf[t, ty, i].reshape(2 * SHARE, D), rows[t, first:first + size, :], (((1,), (1,)), ((), ())),
            preferred_element_type=F32)
        m = jnp.max(s, axis=0, keepdims=True)
        p = jnp.exp(s - m)
        mst[pl.ds(ty * 4 + i, 1), first:first + size] = m
        lst[pl.ds(ty * 4 + i, 1), first:first + size] = jnp.sum(p, axis=0, keepdims=True)
        pbuf[ty, i, :, :, first:first + size] = p.astype(BF16).reshape(2, SHARE, size)

    def near_first(j):
        return j + j // 2 - 2 * (j // 3)

    def normalise(t):
        m = mst[...]
        top = jnp.max(m, axis=0, keepdims=True)
        low = jnp.sum(lst[...] * jnp.exp(m - top), axis=0, keepdims=True)
        places = [pl.ds(pl.multiple_of((z + NZ + off) % NZ * OWN, OWN), OWN) for off in OWNERS]
        for b, where in enumerate(places):
            stats[t, z, 0:1, where] = top[:, b * OWN:(b + 1) * OWN]
            stats[t, z, 1:2, where] = low[:, b * OWN:(b + 1) * OWN]
        group, sem = sender(), take(1)
        for d in (4, 3, 5, 2, 6, 1, 7):
            copy(stats.at[t, z], stats.at[t, z], zpeer(d), group, sem).start()
        wait_arrived(stats.at[t, pl.ds(0, NZ - 1)], sem)
        wait_sent(stats.at[t, pl.ds(0, NZ - 1)], group)
        peak = stats[t, 0, 0:1, :]
        for i in range(1, NZ):
            peak = jnp.maximum(peak, stats[t, i, 0:1, :])
        total = jnp.zeros_like(peak)
        for i in range(NZ):
            total = total + stats[t, i, 1:2, :] * jnp.exp(stats[t, i, 0:1, :] - peak)
        joint[0:1, :] = peak
        joint[1:2, :] = total
        for b, where in enumerate(places):
            joint[2:4, b * OWN:(b + 1) * OWN] = joint[0:2, where]
        mst[...] = jnp.exp(m - joint[2:3, :]) / joint[3:4, :]

    core_from, plane_from, second_from, mass_from = sender(), sender(), sender(), sender()
    core_sem, onward_sem, plane_sem, second_sem, mass_sem = take(8), take(2), take(2), take(2), take(3)

    def reduce_sums(t, midway):

        def core_copy(ty, j):
            i = target(ty, j)
            return copy(sums.at[ty, i, 1 - k], crecv.at[t, ty, i], other, core_from, core_sem + ty * 4 + j)

        def part_of(half):
            return pl.ds(pl.multiple_of(half * (SHARE // 2), SHARE // 2), SHARE // 2)

        def plane_copy(ty, d, target_of, half, dst, sem):
            c = x + ty * (y - x)
            i = (c + d) % 4
            to = at(x + (1 - ty) * (i - x), y + ty * (i - y), z, k)
            return copy(abuf.at[t, ty, (c + target_of) % 4, part_of(half)], dst, to, plane_from, sem + ty)

        def onward_copy(ty, half):
            return plane_copy(ty, 1 + 2 * half, 2, half, onward.at[t, ty, half], onward_sem)

        def last_copy(ty, d, half):
            return plane_copy(ty, d, d, half, arecv.at[t, ty, d // 2, part_of(half)], plane_sem)

        def far_first(j):
            return (2 + j * (j + 1) // 2) % 4

        def target(ty, j):
            return (x + ty * (y - x) + far_first(j)) % 4

        def combine(n):
            ty, j = n % 2, n // 2
            i = target(ty, j)
            core_copy(ty, j).wait_recv()
            whole = sums[ty, i, k] + crecv[t, ty, i]
            sums[ty, i, k] = whole
            abuf[t, ty, i] = whole.astype(BF16)

            @pl.when(j == 0)
            def _():
                onward_copy(ty, 0).start()
                onward_copy(ty, 1).start()

            @pl.when((j == 1) | (j == 2))
            def _():
                last_copy(ty, far_first(j), j - 1).start()

        def body(n, _):
            ty, j = n % 2, n // 2
            i = target(ty, j)
            f = mst[pl.ds(ty * 4 + i, 1), :]
            for h in range(2):
                pbuf[ty, i, h] = (pbuf[ty, i, h].astype(F32) * f).astype(BF16)
            both = jnp.dot(pbuf[ty, i].reshape(2 * SHARE, ROWS), rows[t], preferred_element_type=F32)
            sums[ty, i] = both.reshape(2, SHARE, D)
            core_copy(ty, j).start()

            @pl.when(n > 1)
            def _():
                combine(n - 2)

            return 0

        lax.fori_loop(0, 8, body, 0)
        combine(6)
        combine(7)
        for ty in range(2):
            wait_arrived(lines(SHARE), onward_sem + ty)
            for half, d in ((0, 1), (1, 3)):
                i = (me[ty] + d) % 4
                piece = slice(half * (SHARE // 2), (half + 1) * (SHARE // 2))
                abuf[t, ty, i, piece, :] = (sums[ty, i, k, piece, :] + onward[t, ty, half].astype(F32)).astype(BF16)
                last_copy(ty, d, half).start()

        def masses(n, _):
            ty, i = n // 4, n % 4
            for h in range(2):
                wide = pbuf[ty, i, h].astype(F32)
                acc = wide[:, :128]
                for b in range(1, ROWS // 128):
                    acc = acc + wide[:, b * 128:(b + 1) * 128]
                gbuf[ty, i, h] = jnp.broadcast_to(jnp.sum(acc.T, axis=0, keepdims=True), (8, SHARE))
            return 0

        lax.fori_loop(0, 8, masses, 0)
        for h in range(2):
            for b in range(NX):
                for q in range(NY):
                    glin[t, h, b, :, q * QUART:q * QUART + ITEM] = gbuf[0, b, h, :, q * ITEM:(q + 1) * ITEM]
                    glin[t, h, b, :, q * QUART + ITEM:(q + 1) * QUART] = gbuf[1, q, h, :, b * ITEM:(b + 1) * ITEM]
        g_core = copy(glin.at[t, 1 - k], grecv.at[t], other, mass_from, mass_sem)
        g_core.start()
        g_core.wait()
        for c in range(NX):
            gsum[t, c] = glin[t, k, c] + grecv[t, c]
        for d in range(1, NX):
            copy(gsum.at[t, (x + d) % NX], g1recv.at[t, d - 1], xpeer(d), mass_from, mass_sem + 1).start()

        for ty in range(2):
            wait_arrived(lines(2 * SHARE), plane_sem + ty)
            part = sums[ty, me[ty], k]
            for n in range(2):
                part = part + arecv[t, ty, n].astype(F32)
            a2f[ty] = part.reshape(4, ITEM, D)
            a2[t, ty] = part.astype(BF16).reshape(4, ITEM, D)
            for d in (2, 1, 3):
                copy(a2.at[t, ty, (me[1 - ty] + d) % 4], a2recv.at[t, ty, d - 1], peer[1 - ty](d),
                     second_from, second_sem + ty).start()
        midway()
        wait_arrived(g1recv.at[t], mass_sem + 1)
        wait_sent(g1recv.at[t], mass_from)
        g = gsum[t, x]
        for n in range(NX - 1):
            g = g + g1recv[t, n]
        g2[t] = g
        for d in range(1, NY):
            copy(g2.at[t], g2recv.at[t, d - 1], ypeer(d), mass_from, mass_sem + 2).start()
        quarter = []
        for ty in range(2):
            wait_arrived(lines(3 * ITEM), second_sem + ty)
            whole = a2f[ty, me[1 - ty]]
            for n in range(3):
                whole = whole + a2recv[t, ty, n].astype(F32)
            quarter.append(whole)
        wait_arrived(g2recv.at[t], mass_sem + 2)
        wait_sent(g2recv.at[t], mass_from)
        for n in range(NY - 1):
            g = g + g2recv[t, n]
        wait_sent(sums.at[0], core_from)
        wait_sent(lines(6 * SHARE), plane_from)
        wait_sent(lines(6 * ITEM), second_from)
        return jnp.concatenate(quarter, axis=0), g

    place = pl.ds(pl.multiple_of(k * PART + y * QUART, QUART), QUART)
    quarter = pl.ds(pl.multiple_of(y * QUART, QUART), QUART)
    lane = lax.broadcasted_iota(jnp.int32, (QUART, PART), 1)
    line = lax.broadcasted_iota(jnp.int32, (QUART, PART), 0) + y * QUART
    hit = lane == line

    def column(v):
        return jnp.sum(jnp.where(hit, v[0:1, :], 0.0), axis=1, keepdims=True)

    def update(old, mass, total, g):
        m = column(mass)
        return (m * old + total) / (m + column(g))

    hop, finish = ring(0, 2)
    hop2, finish2 = ring(1, 2)
    begin, go_on, arrive, on, finish_spread = spread(0)
    hop(1)
    begin((1,))
    go_on((0, 1), (1,))
    hop(2)
    arrive(0, True)
    arrive(1, False)
    arrive(3, False)
    hop(3)
    arrive(2, False)
    hop(4)

    def early(b):
        first, size = b * 2 * OWN, 2 * OWN

        def some(ty, _):
            s = lax.dot_general(
                cbuf[0, ty].reshape(8 * SHARE, D), rows[0, first:first + size, :], (((1,), (1,)), ((), ())),
                preferred_element_type=F32)
            for i in range(4):
                part = s[i * 2 * SHARE:(i + 1) * 2 * SHARE]
                m = jnp.max(part, axis=0, keepdims=True)
                p = jnp.exp(part - m)
                mst[pl.ds(ty * 4 + i, 1), first:first + size] = m
                lst[pl.ds(ty * 4 + i, 1), first:first + size] = jnp.sum(p, axis=0, keepdims=True)
                pbuf[ty, i, :, :, first:first + size] = p.astype(BF16).reshape(2, SHARE, size)
            return 0

        lax.fori_loop(0, 2, some, 0)

    for d in (0, 1, 3, 2):
        for ty in range(2):
            on(ty, d).wait_recv()
    early(0)
    early(1)
    finish(3)
    early(2)
    finish()
    early(3)
    finish_spread((1,))
    normalise(0)
    hop2(1)
    total, g = reduce_sums(0, lambda: hop2(2))
    mass = jnp.broadcast_to(counts[pl.ds(pl.multiple_of(k * PART, PART), PART)].reshape(1, PART), (8, PART))
    fresh = update(cents[quarter, :], mass, total, g)
    cur[...] = fresh
    massbuf[0, k] = mass + g
    fresh = (fresh * SHARP).astype(BF16)
    cbuf[1, 0, x, k, items(y), :] = fresh[:ITEM]
    cbuf[1, 1, y, k, items(x), :] = fresh[ITEM:]
    begin, go_on, arrive, on, finish_spread = spread(1)
    begin((0, 1))
    hop2(3)
    go_on((0, 1), (0, 1))
    hop2(4)
    finish2()

    def late(j, _):
        d = near_first(j)

        @pl.when(j == 0)
        def _():
            arrive(d, True)

        @pl.when((j > 0) & (j < 4))
        def _():
            arrive(d, False)

        @pl.when(j > 0)
        def _():
            before = near_first(j - 1)
            for ty in range(2):
                on(ty, before).wait_recv()
                score(1, ty, (me[ty] + 4 - before) % 4, 0, ROWS)

        return 0

    lax.fori_loop(0, 5, late, 0)
    finish_spread((0, 1))
    normalise(1)
    total, g = reduce_sums(1, lambda: None)
    mass = massbuf[0, k]
    out[place, :] = update(cur[...], mass, total, g).astype(BF16)
    from_final, from_passed, from_mass = sender(), sender(), sender()
    final_sem, passed_sem, new_sem = take(3), take(1), take(1)

    def pass_on(d):
        src = out.at[pl.ds(pl.multiple_of(k * PART + ((y + NY - d) % NY) * QUART, QUART), QUART)]
        copy(src, src, other, from_passed, passed_sem).start()

    for d in (2, 1, 3):
        copy(out.at[place], out.at[place], ypeer(d), from_final, final_sem + d - 1).start()
    pass_on(0)
    massbuf[1, k] = mass + g
    copy(massbuf.at[1, k], massbuf.at[1, k], other, from_mass, new_sem).start()
    for d in (1, 3, 2):
        wait_arrived(out.at[place], final_sem + d - 1)
        pass_on(d)
    wait_arrived(out.at[pl.ds(0, 4 * QUART)], passed_sem)
    wait_arrived(massbuf.at[1, k], new_sem)
    for h in range(2):
        new_counts[h * PART:(h + 1) * PART] = massbuf[1, h][0]
    wait_sent(out.at[pl.ds(0, 3 * QUART)], from_final)
    wait_sent(out.at[pl.ds(0, 4 * QUART)], from_passed)
    wait_sent(massbuf.at[1, 0], from_mass)
    assert used[0] <= SENDS and used[1] <= RECVS, used


def body(batch, centroids, counts):
    vmem = pl.BlockSpec(memory_space=pltpu.VMEM)
    refined, mass = pl.pallas_call(
        kernel,
        out_shape=(
            jax.ShapeDtypeStruct((BLOCK, D), BF16),
            jax.ShapeDtypeStruct((BLOCK,), F32),
        ),
        in_specs=[pl.BlockSpec(memory_space=pltpu.HBM)] * 3,
        out_specs=(vmem, vmem),
        scratch_shapes=[
            pltpu.VMEM((2, ROWS, D), BF16),
            pltpu.VMEM((2, 2, 4, 2, SHARE, D), BF16),
            pltpu.VMEM((2, 4, 2, SHARE, ROWS), BF16),
            pltpu.VMEM((8, ROWS), F32),
            pltpu.VMEM((8, ROWS), F32),
            pltpu.VMEM((2, NZ, 2, ROWS), F32),
            pltpu.VMEM((4, ROWS), F32),
            pltpu.VMEM((2, 4, 2, SHARE, D), F32),
            pltpu.VMEM((2, 2, 4, SHARE, D), F32),
            pltpu.VMEM((2, 2, 4, SHARE, D), BF16),
            pltpu.VMEM((2, 2, 2, SHARE, D), BF16),
            pltpu.VMEM((2, 2, 2, SHARE // 2, D), BF16),
            pltpu.VMEM((2, 2, 4, ITEM, D), BF16),
            pltpu.VMEM((2, 4, ITEM, D), F32),
            pltpu.VMEM((2, 2, 3, ITEM, D), BF16),
            pltpu.VMEM((2, 4, 2, 8, SHARE), F32),
            pltpu.VMEM((2, 2, NX, 8, PART), F32),
            pltpu.VMEM((2, NX, 8, PART), F32),
            pltpu.VMEM((2, NX, 8, PART), F32),
            pltpu.VMEM((2, NX - 1, 8, PART), F32),
            pltpu.VMEM((2, 8, PART), F32),
            pltpu.VMEM((2, NY - 1, 8, PART), F32),
            pltpu.VMEM((QUART, D), F32),
            pltpu.VMEM((2, 2, 8, PART), F32),
            pltpu.VMEM((PART, D), F32),
            pltpu.VMEM((BLOCK,), F32),
            pltpu.SemaphoreType.DMA((4,)),
            pltpu.SemaphoreType.DMA((SENDS,)),
            pltpu.SemaphoreType.DMA((RECVS,)),
        ],
        compiler_params=pltpu.CompilerParams(
            collective_id=0, has_side_effects=True, vmem_limit_bytes=58 * 1024 * 1024
        ),
    )(batch, centroids, counts)
    return refined.astype(F32), mass


def solution(mesh):
    return jax.shard_map(
        body,
        mesh=mesh,
        in_specs=(P(None, ("dp", "cent"), None), P("cent", None), P("cent")),
        out_specs=(P("cent", None), P("cent")),
        check_vma=False,
    )
```

```python
import jax
import jax.numpy as jnp
from jax import lax
from jax.experimental import pallas as pl
from jax.experimental.pallas import tpu as pltpu
from jax.sharding import PartitionSpec as P

MESH = pl.DeviceIdType.MESH
F32 = jnp.float32
BF16 = jnp.bfloat16
SHARP = 4.0

NX, NY, NZ = 4, 4, 8
OWN = 128
ROWS = NZ * OWN
D = 768
BLOCK = 512
PART = BLOCK // 2
QUART = PART // NY
ITEM = QUART // 2
SHARE = 4 * ITEM
SENDS, RECVS = 20, 80
OWNERS = (-1, 1, -2, 2, -3, 3, 0, 4)


def kernel(batch, cents_hbm, counts_hbm, out, new_counts, rows, cbuf, pbuf, mst, lst, stats, joint, sums, crecv, abuf, arecv, onward,
           a2, a2f, a2recv, gbuf, glin, grecv, gsum, g1recv, g2, g2recv, cur, massbuf, cents, counts, load_sem,
           send_sem, recv_sem):
    dp = lax.axis_index("dp")
    ce = lax.axis_index("cent")
    y, k = dp // 2, dp % 2
    x, z = ce // NZ, ce % NZ
    me = (x, y)

    def at(px, py, pz, pk):
        return (py * 2 + pk, px * NZ + pz)

    other = at(x, y, z, 1 - k)

    def xpeer(d):
        return at((x + d) % NX, y, z, k)

    def ypeer(d):
        return at(x, (y + d) % NY, z, k)

    def zpeer(d):
        return at(x, y, (z + d) % NZ, k)

    peer = (xpeer, ypeer)
    used = [0, 0]

    def take(n):
        used[1] += n
        return used[1] - n

    def sender():
        used[0] += 1
        return used[0] - 1

    def copy(src, dst, to, group, sem):
        return pltpu.make_async_remote_copy(
            src_ref=src, dst_ref=dst, send_sem=send_sem.at[group], recv_sem=recv_sem.at[sem],
            device_id=to, device_id_type=MESH)

    def wait_sent(size, group):
        copy(size, size, other, group, 0).wait_send()

    def wait_arrived(size, sem):
        copy(size, size, other, 0, sem).wait_recv()

    def lines(n):
        return rows.at[0, pl.ds(0, n)]

    def items(i):
        return pl.ds(pl.multiple_of(i * ITEM, ITEM), ITEM)

    def slot(h, sign):
        return {0: 6, 4: 7}.get(h, 2 * h - 2 + (sign < 0)) * OWN

    core_half = pl.ds(pl.multiple_of(k * PART, PART), PART)
    own_rows = pl.ds(slot(0, 1), OWN)
    loads = [
        pltpu.make_async_copy(cents_hbm.at[core_half], cents, load_sem.at[0]),
        pltpu.make_async_copy(batch.at[0], rows.at[0, own_rows], load_sem.at[1]),
        pltpu.make_async_copy(batch.at[1], rows.at[1, own_rows], load_sem.at[2]),
        pltpu.make_async_copy(counts_hbm, counts, load_sem.at[3]),
    ]
    for c in loads:
        c.start()

    barrier = pltpu.get_barrier_semaphore()
    peers = [other]
    peers += [xpeer(d) for d in range(1, NX)]
    peers += [ypeer(d) for d in range(1, NY)]
    peers += [zpeer(d) for d in (1, NZ - 1)]
    for p in peers:
        pl.semaphore_signal(barrier, inc=1, device_id=p, device_id_type=MESH)

    loads[0].wait()

    def from_block(first):
        return (cents[pl.ds(pl.multiple_of(first, ITEM), ITEM), :] * SHARP).astype(BF16)

    for q in range(NY):
        cbuf[0, 0, x, k, q * ITEM:(q + 1) * ITEM, :] = from_block(q * QUART)
    cbuf[0, 1, y, k, items(x), :] = from_block(y * QUART + ITEM)

    for c in loads[1:]:
        c.wait()
    pl.semaphore_wait(barrier, len(peers))

    ring_from, ring_sem = sender(), take(14)

    def ring(t, parts):
        size = OWN // parts
        arrived = {}
        count = [0]

        def hop(h):
            for c in range(parts):
                for sign in (1, -1):
                    if h == 4 and (c >= parts // 2) != (sign < 0):
                        continue
                    if h > 1:
                        arrived.pop((h - 1, c, sign)).wait_recv()
                    src = pl.ds(slot(h - 1, sign) + c * size, size)
                    dst = pl.ds(slot(h, sign) + c * size, size)
                    going = copy(rows.at[t, src], rows.at[t, dst], zpeer(sign % NZ), ring_from, ring_sem + count[0])
                    going.start()
                    count[0] += 1
                    arrived[(h, c, sign)] = going

        def finish(last=4):
            for key in sorted(arrived):
                if key[0] <= last:
                    arrived.pop(key).wait_recv()
            if last == 4:
                wait_sent(lines(7 * OWN), ring_from)

        return hop, finish

    near_from, far_from, over_from = sender(), sender(), sender()
    near_sem, far_sem, two_sem, over_sem = take(2), take(16), take(2), take(8)

    def spread(t):
        def near(ty, n):
            src = cbuf.at[t, ty, me[ty], k, items(me[1 - ty])]
            return copy(src, src, peer[1 - ty](n), near_from, near_sem + ty)

        def far(ty, n, d):
            src = cbuf.at[t, ty, me[ty], k, items((me[1 - ty] + 4 - n) % 4)]
            return copy(src, src, peer[ty](d), far_from, far_sem + ty * 8 + d // 2 * 4 + n)

        def further(ty, n, d):
            first = (me[1 - ty] + 4 - n) % 4 * ITEM + d // 2 * (ITEM // 2)
            where = pl.ds(pl.multiple_of(first, ITEM // 2), ITEM // 2)
            src = cbuf.at[t, ty, (me[ty] + 4 - d) % 4, k, where]
            return copy(src, src, peer[ty](d), far_from, two_sem + ty)

        def on(ty, d):
            src = cbuf.at[t, ty, (me[ty] + 4 - d) % 4, k]
            return copy(src, src, other, over_from, over_sem + ty * 4 + d)

        def begin(types):
            for ty in types:
                for n in (2, 1, 3):
                    near(ty, n).start()
            for ty in range(2):
                for d in (1, 3):
                    far(ty, 0, d).start()

        def go_on(types, come):
            for ty in come:
                wait_arrived(lines(3 * ITEM), near_sem + ty)
            for n in (1, 3, 2):
                for d in (1, 3):
                    for ty in types:
                        far(ty, n, d).start()

        def relay(n):
            for ty in range(2):
                for d in (1, 3):
                    wait_arrived(lines(ITEM), far_sem + ty * 8 + d // 2 * 4 + n)
                    further(ty, n, d).start()

        def arrive(d):
            for ty in range(2):
                if d == 2:
                    wait_arrived(lines(SHARE), two_sem + ty)
                on(ty, d).start()

        def finish(types):
            wait_sent(lines(3 * ITEM * len(types)), near_from)
            wait_sent(lines(6 * SHARE), far_from)
            wait_sent(lines(8 * SHARE), over_from)

        return begin, go_on, relay, arrive, on, finish

    def score(t, ty, i, first, size):
        s = lax.dot_general(
            cbuf[t, ty, i].reshape(2 * SHARE, D), rows[t, first:first + size, :], (((1,), (1,)), ((), ())),
            preferred_element_type=F32)
        m = jnp.max(s, axis=0, keepdims=True)
        p = jnp.exp(s - m)
        mst[pl.ds(ty * 4 + i, 1), first:first + size] = m
        lst[pl.ds(ty * 4 + i, 1), first:first + size] = jnp.sum(p, axis=0, keepdims=True)
        pbuf[ty, i, :, :, first:first + size] = p.astype(BF16).reshape(2, SHARE, size)

    def near_first(j):
        return j + j // 2 - 2 * (j // 3)

    def normalise(t):
        m = mst[...]
        top = jnp.max(m, axis=0, keepdims=True)
        low = jnp.sum(lst[...] * jnp.exp(m - top), axis=0, keepdims=True)
        places = [pl.ds(pl.multiple_of((z + NZ + off) % NZ * OWN, OWN), OWN) for off in OWNERS]
        for b, where in enumerate(places):
            stats[t, z, 0:1, where] = top[:, b * OWN:(b + 1) * OWN]
            stats[t, z, 1:2, where] = low[:, b * OWN:(b + 1) * OWN]
        group, sem = sender(), take(1)
        for d in (4, 3, 5, 2, 6, 1, 7):
            copy(stats.at[t, z], stats.at[t, z], zpeer(d), group, sem).start()
        wait_arrived(stats.at[t, pl.ds(0, NZ - 1)], sem)
        wait_sent(stats.at[t, pl.ds(0, NZ - 1)], group)
        peak = stats[t, 0, 0:1, :]
        for i in range(1, NZ):
            peak = jnp.maximum(peak, stats[t, i, 0:1, :])
        total = jnp.zeros_like(peak)
        for i in range(NZ):
            total = total + stats[t, i, 1:2, :] * jnp.exp(stats[t, i, 0:1, :] - peak)
        joint[0:1, :] = peak
        joint[1:2, :] = total
        for b, where in enumerate(places):
            joint[2:4, b * OWN:(b + 1) * OWN] = joint[0:2, where]
        mst[...] = jnp.exp(m - joint[2:3, :]) / joint[3:4, :]

    core_from, plane_from, second_from, mass_from = sender(), sender(), sender(), sender()
    core_sem, onward_sem, plane_sem, second_sem, mass_sem = take(8), take(2), take(2), take(2), take(3)

    def reduce_sums(t, midway):

        def core_copy(ty, j):
            i = target(ty, j)
            return copy(sums.at[ty, i, 1 - k], crecv.at[t, ty, i], other, core_from, core_sem + ty * 4 + j)

        def part_of(half):
            return pl.ds(pl.multiple_of(half * (SHARE // 2), SHARE // 2), SHARE // 2)

        def plane_copy(ty, d, target_of, half, dst, sem):
            c = x + ty * (y - x)
            i = (c + d) % 4
            to = at(x + (1 - ty) * (i - x), y + ty * (i - y), z, k)
            return copy(abuf.at[t, ty, (c + target_of) % 4, part_of(half)], dst, to, plane_from, sem + ty)

        def onward_copy(ty, half):
            return plane_copy(ty, 1 + 2 * half, 2, half, onward.at[t, ty, half], onward_sem)

        def last_copy(ty, d, half):
            return plane_copy(ty, d, d, half, arecv.at[t, ty, d // 2, part_of(half)], plane_sem)

        def far_first(j):
            return (2 + j * (j + 1) // 2) % 4

        def target(ty, j):
            return (x + ty * (y - x) + far_first(j)) % 4

        def combine(n):
            ty, j = n % 2, n // 2
            i = target(ty, j)
            core_copy(ty, j).wait_recv()
            whole = sums[ty, i, k] + crecv[t, ty, i]
            sums[ty, i, k] = whole
            abuf[t, ty, i] = whole.astype(BF16)

            @pl.when(j == 0)
            def _():
                onward_copy(ty, 0).start()
                onward_copy(ty, 1).start()

            @pl.when((j == 1) | (j == 2))
            def _():
                last_copy(ty, far_first(j), j - 1).start()

        def body(n, _):
            ty, j = n % 2, n // 2
            i = target(ty, j)
            f = mst[pl.ds(ty * 4 + i, 1), :]
            for h in range(2):
                pbuf[ty, i, h] = (pbuf[ty, i, h].astype(F32) * f).astype(BF16)
            both = jnp.dot(pbuf[ty, i].reshape(2 * SHARE, ROWS), rows[t], preferred_element_type=F32)
            sums[ty, i] = both.reshape(2, SHARE, D)
            core_copy(ty, j).start()

            @pl.when(n > 1)
            def _():
                combine(n - 2)

            return 0

        lax.fori_loop(0, 8, body, 0)
        combine(6)
        combine(7)
        for ty in range(2):
            wait_arrived(lines(SHARE), onward_sem + ty)
            for half, d in ((0, 1), (1, 3)):
                i = (me[ty] + d) % 4
                piece = slice(half * (SHARE // 2), (half + 1) * (SHARE // 2))
                abuf[t, ty, i, piece, :] = (sums[ty, i, k, piece, :] + onward[t, ty, half].astype(F32)).astype(BF16)
                last_copy(ty, d, half).start()

        def masses(n, _):
            ty, i = n // 4, n % 4
            for h in range(2):
                wide = pbuf[ty, i, h].astype(F32)
                acc = wide[:, :128]
                for b in range(1, ROWS // 128):
                    acc = acc + wide[:, b * 128:(b + 1) * 128]
                gbuf[ty, i, h] = jnp.broadcast_to(jnp.sum(acc.T, axis=0, keepdims=True), (8, SHARE))
            return 0

        lax.fori_loop(0, 8, masses, 0)
        for h in range(2):
            for b in range(NX):
                for q in range(NY):
                    glin[t, h, b, :, q * QUART:q * QUART + ITEM] = gbuf[0, b, h, :, q * ITEM:(q + 1) * ITEM]
                    glin[t, h, b, :, q * QUART + ITEM:(q + 1) * QUART] = gbuf[1, q, h, :, b * ITEM:(b + 1) * ITEM]
        g_core = copy(glin.at[t, 1 - k], grecv.at[t], other, mass_from, mass_sem)
        g_core.start()
        g_core.wait()
        for c in range(NX):
            gsum[t, c] = glin[t, k, c] + grecv[t, c]
        for d in range(1, NX):
            copy(gsum.at[t, (x + d) % NX], g1recv.at[t, d - 1], xpeer(d), mass_from, mass_sem + 1).start()

        for ty in range(2):
            wait_arrived(lines(2 * SHARE), plane_sem + ty)
            part = sums[ty, me[ty], k]
            for n in range(2):
                part = part + arecv[t, ty, n].astype(F32)
            a2f[ty] = part.reshape(4, ITEM, D)
            a2[t, ty] = part.astype(BF16).reshape(4, ITEM, D)
            for d in (2, 1, 3):
                copy(a2.at[t, ty, (me[1 - ty] + d) % 4], a2recv.at[t, ty, d - 1], peer[1 - ty](d),
                     second_from, second_sem + ty).start()
        midway()
        wait_arrived(g1recv.at[t], mass_sem + 1)
        wait_sent(g1recv.at[t], mass_from)
        g = gsum[t, x]
        for n in range(NX - 1):
            g = g + g1recv[t, n]
        g2[t] = g
        for d in range(1, NY):
            copy(g2.at[t], g2recv.at[t, d - 1], ypeer(d), mass_from, mass_sem + 2).start()
        quarter = []
        for ty in range(2):
            wait_arrived(lines(3 * ITEM), second_sem + ty)
            whole = a2f[ty, me[1 - ty]]
            for n in range(3):
                whole = whole + a2recv[t, ty, n].astype(F32)
            quarter.append(whole)
        wait_arrived(g2recv.at[t], mass_sem + 2)
        wait_sent(g2recv.at[t], mass_from)
        for n in range(NY - 1):
            g = g + g2recv[t, n]
        wait_sent(sums.at[0], core_from)
        wait_sent(lines(6 * SHARE), plane_from)
        wait_sent(lines(6 * ITEM), second_from)
        return jnp.concatenate(quarter, axis=0), g

    place = pl.ds(pl.multiple_of(k * PART + y * QUART, QUART), QUART)
    quarter = pl.ds(pl.multiple_of(y * QUART, QUART), QUART)
    lane = lax.broadcasted_iota(jnp.int32, (QUART, PART), 1)
    line = lax.broadcasted_iota(jnp.int32, (QUART, PART), 0) + y * QUART
    hit = lane == line

    def column(v):
        return jnp.sum(jnp.where(hit, v[0:1, :], 0.0), axis=1, keepdims=True)

    def update(old, mass, total, g):
        m = column(mass)
        return (m * old + total) / (m + column(g))

    hop, finish = ring(0, 2)
    hop2, finish2 = ring(1, 2)
    begin, go_on, relay, arrive, on, finish_spread = spread(0)
    hop(1)
    begin((1,))
    go_on((0, 1), (1,))
    hop(2)
    relay(0)
    arrive(0)
    for n in (1, 3, 2):
        relay(n)
    arrive(1)
    arrive(3)
    hop(3)
    arrive(2)
    hop(4)

    def early(b):
        first, size = b * 2 * OWN, 2 * OWN

        def some(ty, _):
            s = lax.dot_general(
                cbuf[0, ty].reshape(8 * SHARE, D), rows[0, first:first + size, :], (((1,), (1,)), ((), ())),
                preferred_element_type=F32)
            for i in range(4):
                part = s[i * 2 * SHARE:(i + 1) * 2 * SHARE]
                m = jnp.max(part, axis=0, keepdims=True)
                p = jnp.exp(part - m)
                mst[pl.ds(ty * 4 + i, 1), first:first + size] = m
                lst[pl.ds(ty * 4 + i, 1), first:first + size] = jnp.sum(p, axis=0, keepdims=True)
                pbuf[ty, i, :, :, first:first + size] = p.astype(BF16).reshape(2, SHARE, size)
            return 0

        lax.fori_loop(0, 2, some, 0)

    for d in (0, 1, 3, 2):
        for ty in range(2):
            on(ty, d).wait_recv()
    early(0)
    early(1)
    finish(3)
    early(2)
    finish()
    early(3)
    finish_spread((1,))
    normalise(0)
    hop2(1)
    total, g = reduce_sums(0, lambda: hop2(2))
    mass = jnp.broadcast_to(counts[pl.ds(pl.multiple_of(k * PART, PART), PART)].reshape(1, PART), (8, PART))
    fresh = update(cents[quarter, :], mass, total, g)
    cur[...] = fresh
    massbuf[0, k] = mass + g
    fresh = (fresh * SHARP).astype(BF16)
    cbuf[1, 0, x, k, items(y), :] = fresh[:ITEM]
    cbuf[1, 1, y, k, items(x), :] = fresh[ITEM:]
    begin, go_on, relay, arrive, on, finish_spread = spread(1)
    begin((0, 1))
    hop2(3)
    go_on((0, 1), (0, 1))
    arrive(0)
    relay(0)
    hop2(4)
    for n in (1, 3, 2):
        relay(n)
    arrive(1)
    arrive(3)
    finish2()

    def late(j, _):
        d = near_first(j)

        @pl.when(j == 3)
        def _():
            arrive(2)

        for ty in range(2):
            on(ty, d).wait_recv()
            score(1, ty, (me[ty] + 4 - d) % 4, 0, ROWS)
        return 0

    lax.fori_loop(0, 4, late, 0)
    finish_spread((0, 1))
    normalise(1)
    total, g = reduce_sums(1, lambda: None)
    mass = massbuf[0, k]
    out[place, :] = update(cur[...], mass, total, g).astype(BF16)
    from_final, from_passed, from_mass = sender(), sender(), sender()
    final_sem, passed_sem, new_sem = take(3), take(1), take(1)

    def pass_on(d):
        src = out.at[pl.ds(pl.multiple_of(k * PART + ((y + NY - d) % NY) * QUART, QUART), QUART)]
        copy(src, src, other, from_passed, passed_sem).start()

    for d in (2, 1, 3):
        copy(out.at[place], out.at[place], ypeer(d), from_final, final_sem + d - 1).start()
    pass_on(0)
    massbuf[1, k] = mass + g
    copy(massbuf.at[1, k], massbuf.at[1, k], other, from_mass, new_sem).start()
    for d in (1, 3, 2):
        wait_arrived(out.at[place], final_sem + d - 1)
        pass_on(d)
    wait_arrived(out.at[pl.ds(0, 4 * QUART)], passed_sem)
    wait_arrived(massbuf.at[1, k], new_sem)
    for h in range(2):
        new_counts[h * PART:(h + 1) * PART] = massbuf[1, h][0]
    wait_sent(out.at[pl.ds(0, 3 * QUART)], from_final)
    wait_sent(out.at[pl.ds(0, 4 * QUART)], from_passed)
    wait_sent(massbuf.at[1, 0], from_mass)
    assert used[0] <= SENDS and used[1] <= RECVS, used


def body(batch, centroids, counts):
    vmem = pl.BlockSpec(memory_space=pltpu.VMEM)
    refined, mass = pl.pallas_call(
        kernel,
        out_shape=(
            jax.ShapeDtypeStruct((BLOCK, D), BF16),
            jax.ShapeDtypeStruct((BLOCK,), F32),
        ),
        in_specs=[pl.BlockSpec(memory_space=pltpu.HBM)] * 3,
        out_specs=(vmem, vmem),
        scratch_shapes=[
            pltpu.VMEM((2, ROWS, D), BF16),
            pltpu.VMEM((2, 2, 4, 2, SHARE, D), BF16),
            pltpu.VMEM((2, 4, 2, SHARE, ROWS), BF16),
            pltpu.VMEM((8, ROWS), F32),
            pltpu.VMEM((8, ROWS), F32),
            pltpu.VMEM((2, NZ, 2, ROWS), F32),
            pltpu.VMEM((4, ROWS), F32),
            pltpu.VMEM((2, 4, 2, SHARE, D), F32),
            pltpu.VMEM((2, 2, 4, SHARE, D), F32),
            pltpu.VMEM((2, 2, 4, SHARE, D), BF16),
            pltpu.VMEM((2, 2, 2, SHARE, D), BF16),
            pltpu.VMEM((2, 2, 2, SHARE // 2, D), BF16),
            pltpu.VMEM((2, 2, 4, ITEM, D), BF16),
            pltpu.VMEM((2, 4, ITEM, D), F32),
            pltpu.VMEM((2, 2, 3, ITEM, D), BF16),
            pltpu.VMEM((2, 4, 2, 8, SHARE), F32),
            pltpu.VMEM((2, 2, NX, 8, PART), F32),
            pltpu.VMEM((2, NX, 8, PART), F32),
            pltpu.VMEM((2, NX, 8, PART), F32),
            pltpu.VMEM((2, NX - 1, 8, PART), F32),
            pltpu.VMEM((2, 8, PART), F32),
            pltpu.VMEM((2, NY - 1, 8, PART), F32),
            pltpu.VMEM((QUART, D), F32),
            pltpu.VMEM((2, 2, 8, PART), F32),
            pltpu.VMEM((PART, D), F32),
            pltpu.VMEM((BLOCK,), F32),
            pltpu.SemaphoreType.DMA((4,)),
            pltpu.SemaphoreType.DMA((SENDS,)),
            pltpu.SemaphoreType.DMA((RECVS,)),
        ],
        compiler_params=pltpu.CompilerParams(
            collective_id=0, has_side_effects=True, vmem_limit_bytes=58 * 1024 * 1024
        ),
    )(batch, centroids, counts)
    return refined.astype(F32), mass


def solution(mesh):
    return jax.shard_map(
        body,
        mesh=mesh,
        in_specs=(P(None, ("dp", "cent"), None), P("cent", None), P("cent")),
        out_specs=(P("cent", None), P("cent")),
        check_vma=False,
    )
```

```python
import jax
import jax.numpy as jnp
from jax import lax
from jax.experimental import pallas as pl
from jax.experimental.pallas import tpu as pltpu
from jax.sharding import PartitionSpec as P

MESH = pl.DeviceIdType.MESH
F32 = jnp.float32
BF16 = jnp.bfloat16
SHARP = 4.0

NX, NY, NZ = 4, 4, 8
OWN = 128
ROWS = NZ * OWN
D = 768
BLOCK = 512
PART = BLOCK // 2
QUART = PART // NY
ITEM = QUART // 2
SHARE = 4 * ITEM
SENDS, RECVS = 20, 80
OWNERS = (-1, 1, -2, 2, -3, 3, 0, 4)


def kernel(batch, cents_hbm, counts_hbm, out, new_counts, rows, cbuf, pbuf, mst, lst, stats, joint, sums, crecv, abuf, arecv, onward,
           a2, a2f, a2recv, gbuf, glin, grecv, gsum, g1recv, g2, g2recv, cur, massbuf, cents, counts, load_sem,
           send_sem, recv_sem):
    dp = lax.axis_index("dp")
    ce = lax.axis_index("cent")
    y, k = dp // 2, dp % 2
    x, z = ce // NZ, ce % NZ
    me = (x, y)

    def at(px, py, pz, pk):
        return (py * 2 + pk, px * NZ + pz)

    other = at(x, y, z, 1 - k)

    def xpeer(d):
        return at((x + d) % NX, y, z, k)

    def ypeer(d):
        return at(x, (y + d) % NY, z, k)

    def zpeer(d):
        return at(x, y, (z + d) % NZ, k)

    peer = (xpeer, ypeer)
    used = [0, 0]

    def take(n):
        used[1] += n
        return used[1] - n

    def sender():
        used[0] += 1
        return used[0] - 1

    def copy(src, dst, to, group, sem):
        return pltpu.make_async_remote_copy(
            src_ref=src, dst_ref=dst, send_sem=send_sem.at[group], recv_sem=recv_sem.at[sem],
            device_id=to, device_id_type=MESH)

    def wait_sent(size, group):
        copy(size, size, other, group, 0).wait_send()

    def wait_arrived(size, sem):
        copy(size, size, other, 0, sem).wait_recv()

    def lines(n):
        return rows.at[0, pl.ds(0, n)]

    def items(i):
        return pl.ds(pl.multiple_of(i * ITEM, ITEM), ITEM)

    def slot(h, sign):
        return {0: 6, 4: 7}.get(h, 2 * h - 2 + (sign < 0)) * OWN

    core_half = pl.ds(pl.multiple_of(k * PART, PART), PART)
    own_rows = pl.ds(slot(0, 1), OWN)
    loads = [
        pltpu.make_async_copy(cents_hbm.at[core_half], cents, load_sem.at[0]),
        pltpu.make_async_copy(batch.at[0], rows.at[0, own_rows], load_sem.at[1]),
        pltpu.make_async_copy(batch.at[1], rows.at[1, own_rows], load_sem.at[2]),
        pltpu.make_async_copy(counts_hbm, counts, load_sem.at[3]),
    ]
    for c in loads:
        c.start()

    barrier = pltpu.get_barrier_semaphore()
    peers = [other]
    peers += [xpeer(d) for d in range(1, NX)]
    peers += [ypeer(d) for d in range(1, NY)]
    peers += [zpeer(d) for d in (1, NZ - 1)]
    for p in peers:
        pl.semaphore_signal(barrier, inc=1, device_id=p, device_id_type=MESH)

    loads[0].wait()

    def from_block(first):
        return (cents[pl.ds(pl.multiple_of(first, ITEM), ITEM), :] * SHARP).astype(BF16)

    for q in range(NY):
        cbuf[0, 0, x, k, q * ITEM:(q + 1) * ITEM, :] = from_block(q * QUART)
    cbuf[0, 1, y, k, items(x), :] = from_block(y * QUART + ITEM)

    for c in loads[1:]:
        c.wait()
    pl.semaphore_wait(barrier, len(peers))

    ring_from, ring_sem = sender(), take(14)

    def ring(t, parts):
        size = OWN // parts
        arrived = {}
        count = [0]

        def hop(h):
            for c in range(parts):
                for sign in (1, -1):
                    if h == 4 and (c >= parts // 2) != (sign < 0):
                        continue
                    if h > 1:
                        arrived.pop((h - 1, c, sign)).wait_recv()
                    src = pl.ds(slot(h - 1, sign) + c * size, size)
                    dst = pl.ds(slot(h, sign) + c * size, size)
                    going = copy(rows.at[t, src], rows.at[t, dst], zpeer(sign % NZ), ring_from, ring_sem + count[0])
                    going.start()
                    count[0] += 1
                    arrived[(h, c, sign)] = going

        def finish(last=4):
            for key in sorted(arrived):
                if key[0] <= last:
                    arrived.pop(key).wait_recv()
            if last == 4:
                wait_sent(lines(7 * OWN), ring_from)

        return hop, finish

    near_from, far_from, over_from = sender(), sender(), sender()
    near_sem, far_sem, two_sem, over_sem = take(2), take(16), take(2), take(8)

    def spread(t):
        def near(ty, n):
            src = cbuf.at[t, ty, me[ty], k, items(me[1 - ty])]
            return copy(src, src, peer[1 - ty](n), near_from, near_sem + ty)

        def far(ty, n, d):
            src = cbuf.at[t, ty, me[ty], k, items((me[1 - ty] + 4 - n) % 4)]
            return copy(src, src, peer[ty](d), far_from, far_sem + ty * 8 + d // 2 * 4 + n)

        def further(ty, n, d):
            first = (me[1 - ty] + 4 - n) % 4 * ITEM + d // 2 * (ITEM // 2)
            where = pl.ds(pl.multiple_of(first, ITEM // 2), ITEM // 2)
            src = cbuf.at[t, ty, (me[ty] + 4 - d) % 4, k, where]
            return copy(src, src, peer[ty](d), far_from, two_sem + ty)

        def on(ty, d):
            src = cbuf.at[t, ty, (me[ty] + 4 - d) % 4, k]
            return copy(src, src, other, over_from, over_sem + ty * 4 + d)

        def begin(types):
            for ty in types:
                for n in (1, 3, 2):
                    near(ty, n).start()
            for ty in range(2):
                for d in (1, 3):
                    far(ty, 0, d).start()

        def go_on(types, come):
            for ty in come:
                wait_arrived(lines(3 * ITEM), near_sem + ty)
            for n in (1, 3, 2):
                for d in (1, 3):
                    for ty in types:
                        far(ty, n, d).start()

        def relay(n):
            for ty in range(2):
                for d in (1, 3):
                    wait_arrived(lines(ITEM), far_sem + ty * 8 + d // 2 * 4 + n)
                    further(ty, n, d).start()

        def arrive(d):
            for ty in range(2):
                if d == 2:
                    wait_arrived(lines(SHARE), two_sem + ty)
                on(ty, d).start()

        def finish(types):
            wait_sent(lines(3 * ITEM * len(types)), near_from)
            wait_sent(lines(6 * SHARE), far_from)
            wait_sent(lines(8 * SHARE), over_from)

        return begin, go_on, relay, arrive, on, finish

    def score(t, ty, i, first, size):
        s = lax.dot_general(
            cbuf[t, ty, i].reshape(2 * SHARE, D), rows[t, first:first + size, :], (((1,), (1,)), ((), ())),
            preferred_element_type=F32)
        m = jnp.max(s, axis=0, keepdims=True)
        p = jnp.exp(s - m)
        mst[pl.ds(ty * 4 + i, 1), first:first + size] = m
        lst[pl.ds(ty * 4 + i, 1), first:first + size] = jnp.sum(p, axis=0, keepdims=True)
        pbuf[ty, i, :, :, first:first + size] = p.astype(BF16).reshape(2, SHARE, size)

    def near_first(j):
        return j + j // 2 - 2 * (j // 3)

    def normalise(t):
        m = mst[...]
        top = jnp.max(m, axis=0, keepdims=True)
        low = jnp.sum(lst[...] * jnp.exp(m - top), axis=0, keepdims=True)
        places = [pl.ds(pl.multiple_of((z + NZ + off) % NZ * OWN, OWN), OWN) for off in OWNERS]
        for b, where in enumerate(places):
            stats[t, z, 0:1, where] = top[:, b * OWN:(b + 1) * OWN]
            stats[t, z, 1:2, where] = low[:, b * OWN:(b + 1) * OWN]
        group, sem = sender(), take(1)
        for d in (4, 3, 5, 2, 6, 1, 7):
            copy(stats.at[t, z], stats.at[t, z], zpeer(d), group, sem).start()
        wait_arrived(stats.at[t, pl.ds(0, NZ - 1)], sem)
        wait_sent(stats.at[t, pl.ds(0, NZ - 1)], group)
        peak = stats[t, 0, 0:1, :]
        for i in range(1, NZ):
            peak = jnp.maximum(peak, stats[t, i, 0:1, :])
        total = jnp.zeros_like(peak)
        for i in range(NZ):
            total = total + stats[t, i, 1:2, :] * jnp.exp(stats[t, i, 0:1, :] - peak)
        joint[0:1, :] = peak
        joint[1:2, :] = total
        for b, where in enumerate(places):
            joint[2:4, b * OWN:(b + 1) * OWN] = joint[0:2, where]
        mst[...] = jnp.exp(m - joint[2:3, :]) / joint[3:4, :]

    core_from, plane_from, second_from, mass_from = sender(), sender(), sender(), sender()
    core_sem, onward_sem, plane_sem, second_sem, mass_sem = take(8), take(2), take(2), take(2), take(3)

    def reduce_sums(t, midway):

        def core_copy(ty, j):
            i = target(ty, j)
            return copy(sums.at[ty, i, 1 - k], crecv.at[t, ty, i], other, core_from, core_sem + ty * 4 + j)

        def part_of(half):
            return pl.ds(pl.multiple_of(half * (SHARE // 2), SHARE // 2), SHARE // 2)

        def plane_copy(ty, d, target_of, half, dst, sem):
            c = x + ty * (y - x)
            i = (c + d) % 4
            to = at(x + (1 - ty) * (i - x), y + ty * (i - y), z, k)
            return copy(abuf.at[t, ty, (c + target_of) % 4, part_of(half)], dst, to, plane_from, sem + ty)

        def onward_copy(ty, half):
            return plane_copy(ty, 1 + 2 * half, 2, half, onward.at[t, ty, half], onward_sem)

        def last_copy(ty, d, half):
            return plane_copy(ty, d, d, half, arecv.at[t, ty, d // 2, part_of(half)], plane_sem)

        def far_first(j):
            return (2 + j * (j + 1) // 2) % 4

        def target(ty, j):
            return (x + ty * (y - x) + far_first(j)) % 4

        def combine(n):
            ty, j = n % 2, n // 2
            i = target(ty, j)
            core_copy(ty, j).wait_recv()
            whole = sums[ty, i, k] + crecv[t, ty, i]
            sums[ty, i, k] = whole
            abuf[t, ty, i] = whole.astype(BF16)

            @pl.when(j == 0)
            def _():
                onward_copy(ty, 0).start()
                onward_copy(ty, 1).start()

            @pl.when((j == 1) | (j == 2))
            def _():
                last_copy(ty, far_first(j), j - 1).start()

        def body(n, _):
            ty, j = n % 2, n // 2
            i = target(ty, j)
            f = mst[pl.ds(ty * 4 + i, 1), :]
            for h in range(2):
                pbuf[ty, i, h] = (pbuf[ty, i, h].astype(F32) * f).astype(BF16)
            both = jnp.dot(pbuf[ty, i].reshape(2 * SHARE, ROWS), rows[t], preferred_element_type=F32)
            sums[ty, i] = both.reshape(2, SHARE, D)
            core_copy(ty, j).start()

            @pl.when(n > 1)
            def _():
                combine(n - 2)

            return 0

        lax.fori_loop(0, 8, body, 0)
        combine(6)
        combine(7)
        for ty in range(2):
            wait_arrived(lines(SHARE), onward_sem + ty)
            for half, d in ((0, 1), (1, 3)):
                i = (me[ty] + d) % 4
                piece = slice(half * (SHARE // 2), (half + 1) * (SHARE // 2))
                abuf[t, ty, i, piece, :] = (sums[ty, i, k, piece, :] + onward[t, ty, half].astype(F32)).astype(BF16)
                last_copy(ty, d, half).start()

        def masses(n, _):
            ty, i = n // 4, n % 4
            for h in range(2):
                wide = pbuf[ty, i, h].astype(F32)
                acc = wide[:, :128]
                for b in range(1, ROWS // 128):
                    acc = acc + wide[:, b * 128:(b + 1) * 128]
                gbuf[ty, i, h] = jnp.broadcast_to(jnp.sum(acc.T, axis=0, keepdims=True), (8, SHARE))
            return 0

        lax.fori_loop(0, 8, masses, 0)
        for h in range(2):
            for b in range(NX):
                for q in range(NY):
                    glin[t, h, b, :, q * QUART:q * QUART + ITEM] = gbuf[0, b, h, :, q * ITEM:(q + 1) * ITEM]
                    glin[t, h, b, :, q * QUART + ITEM:(q + 1) * QUART] = gbuf[1, q, h, :, b * ITEM:(b + 1) * ITEM]
        g_core = copy(glin.at[t, 1 - k], grecv.at[t], other, mass_from, mass_sem)
        g_core.start()
        g_core.wait()
        for c in range(NX):
            gsum[t, c] = glin[t, k, c] + grecv[t, c]
        for d in range(1, NX):
            copy(gsum.at[t, (x + d) % NX], g1recv.at[t, d - 1], xpeer(d), mass_from, mass_sem + 1).start()

        for ty in range(2):
            wait_arrived(lines(2 * SHARE), plane_sem + ty)
            part = sums[ty, me[ty], k]
            for n in range(2):
                part = part + arecv[t, ty, n].astype(F32)
            a2f[ty] = part.reshape(4, ITEM, D)
            a2[t, ty] = part.astype(BF16).reshape(4, ITEM, D)
            for d in (2, 1, 3):
                copy(a2.at[t, ty, (me[1 - ty] + d) % 4], a2recv.at[t, ty, d - 1], peer[1 - ty](d),
                     second_from, second_sem + ty).start()
        midway()
        wait_arrived(g1recv.at[t], mass_sem + 1)
        wait_sent(g1recv.at[t], mass_from)
        g = gsum[t, x]
        for n in range(NX - 1):
            g = g + g1recv[t, n]
        g2[t] = g
        for d in range(1, NY):
            copy(g2.at[t], g2recv.at[t, d - 1], ypeer(d), mass_from, mass_sem + 2).start()
        quarter = []
        for ty in range(2):
            wait_arrived(lines(3 * ITEM), second_sem + ty)
            whole = a2f[ty, me[1 - ty]]
            for n in range(3):
                whole = whole + a2recv[t, ty, n].astype(F32)
            quarter.append(whole)
        wait_arrived(g2recv.at[t], mass_sem + 2)
        wait_sent(g2recv.at[t], mass_from)
        for n in range(NY - 1):
            g = g + g2recv[t, n]
        wait_sent(sums.at[0], core_from)
        wait_sent(lines(6 * SHARE), plane_from)
        wait_sent(lines(6 * ITEM), second_from)
        return jnp.concatenate(quarter, axis=0), g

    place = pl.ds(pl.multiple_of(k * PART + y * QUART, QUART), QUART)
    quarter = pl.ds(pl.multiple_of(y * QUART, QUART), QUART)
    lane = lax.broadcasted_iota(jnp.int32, (QUART, PART), 1)
    line = lax.broadcasted_iota(jnp.int32, (QUART, PART), 0) + y * QUART
    hit = lane == line

    def column(v):
        return jnp.sum(jnp.where(hit, v[0:1, :], 0.0), axis=1, keepdims=True)

    def update(old, mass, total, g):
        m = column(mass)
        return (m * old + total) / (m + column(g))

    hop, finish = ring(0, 2)
    hop2, finish2 = ring(1, 2)
    begin, go_on, relay, arrive, on, finish_spread = spread(0)
    hop(1)
    begin((1,))
    go_on((0, 1), (1,))
    hop(2)
    relay(0)
    arrive(0)
    for n in (1, 3, 2):
        relay(n)
    arrive(1)
    arrive(3)
    hop(3)
    arrive(2)
    hop(4)

    def early(b):
        first, size = b * 2 * OWN, 2 * OWN

        def some(ty, _):
            s = lax.dot_general(
                cbuf[0, ty].reshape(8 * SHARE, D), rows[0, first:first + size, :], (((1,), (1,)), ((), ())),
                preferred_element_type=F32)
            for i in range(4):
                part = s[i * 2 * SHARE:(i + 1) * 2 * SHARE]
                m = jnp.max(part, axis=0, keepdims=True)
                p = jnp.exp(part - m)
                mst[pl.ds(ty * 4 + i, 1), first:first + size] = m
                lst[pl.ds(ty * 4 + i, 1), first:first + size] = jnp.sum(p, axis=0, keepdims=True)
                pbuf[ty, i, :, :, first:first + size] = p.astype(BF16).reshape(2, SHARE, size)
            return 0

        lax.fori_loop(0, 2, some, 0)

    for d in (0, 1, 3, 2):
        for ty in range(2):
            on(ty, d).wait_recv()
    early(0)
    early(1)
    finish(3)
    early(2)
    finish()
    early(3)
    finish_spread((1,))
    normalise(0)
    hop2(1)
    total, g = reduce_sums(0, lambda: hop2(2))
    mass = jnp.broadcast_to(counts[pl.ds(pl.multiple_of(k * PART, PART), PART)].reshape(1, PART), (8, PART))
    fresh = update(cents[quarter, :], mass, total, g)
    cur[...] = fresh
    massbuf[0, k] = mass + g
    fresh = (fresh * SHARP).astype(BF16)
    cbuf[1, 0, x, k, items(y), :] = fresh[:ITEM]
    cbuf[1, 1, y, k, items(x), :] = fresh[ITEM:]
    begin, go_on, relay, arrive, on, finish_spread = spread(1)
    begin((0, 1))
    hop2(3)
    go_on((0, 1), (0, 1))
    arrive(0)
    relay(0)
    hop2(4)
    for n in (1, 3, 2):
        relay(n)
    arrive(1)
    arrive(3)
    finish2()

    def late(j, _):
        d = near_first(j)

        @pl.when(j == 3)
        def _():
            arrive(2)

        for ty in range(2):
            on(ty, d).wait_recv()
            score(1, ty, (me[ty] + 4 - d) % 4, 0, ROWS)
        return 0

    lax.fori_loop(0, 4, late, 0)
    finish_spread((0, 1))
    normalise(1)
    total, g = reduce_sums(1, lambda: None)
    mass = massbuf[0, k]
    out[place, :] = update(cur[...], mass, total, g).astype(BF16)
    from_final, from_passed, from_mass = sender(), sender(), sender()
    final_sem, passed_sem, new_sem = take(3), take(1), take(1)

    def pass_on(d):
        src = out.at[pl.ds(pl.multiple_of(k * PART + ((y + NY - d) % NY) * QUART, QUART), QUART)]
        copy(src, src, other, from_passed, passed_sem).start()

    for d in (2, 1, 3):
        copy(out.at[place], out.at[place], ypeer(d), from_final, final_sem + d - 1).start()
    pass_on(0)
    massbuf[1, k] = mass + g
    copy(massbuf.at[1, k], massbuf.at[1, k], other, from_mass, new_sem).start()
    for d in (1, 3, 2):
        wait_arrived(out.at[place], final_sem + d - 1)
        pass_on(d)
    wait_arrived(out.at[pl.ds(0, 4 * QUART)], passed_sem)
    wait_arrived(massbuf.at[1, k], new_sem)
    for h in range(2):
        new_counts[h * PART:(h + 1) * PART] = massbuf[1, h][0]
    wait_sent(out.at[pl.ds(0, 3 * QUART)], from_final)
    wait_sent(out.at[pl.ds(0, 4 * QUART)], from_passed)
    wait_sent(massbuf.at[1, 0], from_mass)
    assert used[0] <= SENDS and used[1] <= RECVS, used


def body(batch, centroids, counts):
    vmem = pl.BlockSpec(memory_space=pltpu.VMEM)
    refined, mass = pl.pallas_call(
        kernel,
        out_shape=(
            jax.ShapeDtypeStruct((BLOCK, D), BF16),
            jax.ShapeDtypeStruct((BLOCK,), F32),
        ),
        in_specs=[pl.BlockSpec(memory_space=pltpu.HBM)] * 3,
        out_specs=(vmem, vmem),
        scratch_shapes=[
            pltpu.VMEM((2, ROWS, D), BF16),
            pltpu.VMEM((2, 2, 4, 2, SHARE, D), BF16),
            pltpu.VMEM((2, 4, 2, SHARE, ROWS), BF16),
            pltpu.VMEM((8, ROWS), F32),
            pltpu.VMEM((8, ROWS), F32),
            pltpu.VMEM((2, NZ, 2, ROWS), F32),
            pltpu.VMEM((4, ROWS), F32),
            pltpu.VMEM((2, 4, 2, SHARE, D), F32),
            pltpu.VMEM((2, 2, 4, SHARE, D), F32),
            pltpu.VMEM((2, 2, 4, SHARE, D), BF16),
            pltpu.VMEM((2, 2, 2, SHARE, D), BF16),
            pltpu.VMEM((2, 2, 2, SHARE // 2, D), BF16),
            pltpu.VMEM((2, 2, 4, ITEM, D), BF16),
            pltpu.VMEM((2, 4, ITEM, D), F32),
            pltpu.VMEM((2, 2, 3, ITEM, D), BF16),
            pltpu.VMEM((2, 4, 2, 8, SHARE), F32),
            pltpu.VMEM((2, 2, NX, 8, PART), F32),
            pltpu.VMEM((2, NX, 8, PART), F32),
            pltpu.VMEM((2, NX, 8, PART), F32),
            pltpu.VMEM((2, NX - 1, 8, PART), F32),
            pltpu.VMEM((2, 8, PART), F32),
            pltpu.VMEM((2, NY - 1, 8, PART), F32),
            pltpu.VMEM((QUART, D), F32),
            pltpu.VMEM((2, 2, 8, PART), F32),
            pltpu.VMEM((PART, D), F32),
            pltpu.VMEM((BLOCK,), F32),
            pltpu.SemaphoreType.DMA((4,)),
            pltpu.SemaphoreType.DMA((SENDS,)),
            pltpu.SemaphoreType.DMA((RECVS,)),
        ],
        compiler_params=pltpu.CompilerParams(
            collective_id=0, has_side_effects=True, vmem_limit_bytes=58 * 1024 * 1024
        ),
    )(batch, centroids, counts)
    return refined.astype(F32), mass


def solution(mesh):
    return jax.shard_map(
        body,
        mesh=mesh,
        in_specs=(P(None, ("dp", "cent"), None), P("cent", None), P("cent")),
        out_specs=(P("cent", None), P("cent")),
        check_vma=False,
    )
```
